128 devices in a mesh: section: 4 (over z), expert: 32 (over y, x, core).
Axes of the slice: x: 4, y: 4, z: 4, core: 2. Of those that a mesh axis runs over, the one named last changes fastest.
Arguments:
- tokens: bfloat16 [4, 512, 7168], P('section', 'expert'), may hold values from -6 to 6
- norm_gain: float32 [4, 7168], P('section'), may hold values from 0.5 to 1.5
- gate_weight: bfloat16 [4, 7168, 16384], P('section', None, 'expert'), may hold values from -0.0625 to 0.0625
- up_weight: bfloat16 [4, 7168, 16384], P('section', None, 'expert'), may hold values from -0.0625 to 0.0625
- down_weight: bfloat16 [4, 16384, 7168], P('section', 'expert'), may hold values from -0.125 to 0.125
- routes: int32 [4, 4, 512, 2], P('section', None, 'expert'), may hold values from 0 to 7, all different within a row; in each aligned block of 16 rows (0 to 15, 16 to 31, ..., all dimensions but the last counted through in order) at most 6 rows name the same one
- route_weights: float32 [4, 4, 512, 2], P('section', None, 'expert'), may hold values from 0.2 to 1.2
Outputs:
- targets: bfloat16 [4, 512, 7168], P('section', 'expert')
The draws below stay inside these ranges and needn't reach their ends.
Inputs may be any that keep to these rules, and one draw needn't show every extreme that they name: Within the 16 tokens of one device for one layer and micro-batch, no expert is named by more than 6 routes, a bound that some block reaches.
All inputs are finite; a program needn't handle non-finite values.
Results may differ from the reference program's by a relative error of at most 0.019.
Values may be sent and summed in bfloat16 or wider, within the bound.
No kernel may reach another device: no remote copies, remote signals or barrier semaphores. Data moves between devices by JAX's collectives and lax.ppermute only.
A program may use at most 128 MiB of HBM per device.

```python
import math
import jax
import jax.numpy as jnp
import numpy as np
from jax import lax

D = 7168
FFE = 2048
SHARDS = 4
TOPK = 2
MICRO = 4
TOK_DEV = 16
EXPERTS = 8
MB_TOK = 512
CAP = 6
N_SECTION = 4
N_EXPERT = 32


def level_of(stream_key, shape, split, low, high):
    level = 1.0
    for position, shards_of in split:
        steps = jax.random.uniform(jax.random.fold_in(jax.random.fold_in(stream_key, 6), position), (shards_of,), jnp.float32, low / len(split), high / len(split))
        level = level * jnp.repeat(jnp.exp(steps), shape[position] // shards_of).reshape((-1,) + (1,) * (len(shape) - 1 - position))
    return level


def deal_out(stream_key, own, number, rows, amount, top, most, lean):
    ranking = jax.random.permutation(stream_key, amount)
    heavy_load, common = portions_of(amount, rows * top, most, lean, True), portions_of(amount, rows * top, most, lean, False)
    places = jnp.arange(amount)

    def named(lengths, offset_by):
        used = int((lengths > 0).sum())
        fixed = max(1, used // 4)
        moved = fixed + (places - fixed + offset_by * (used - fixed)) % max(1, amount - fixed)
        return jnp.zeros((amount,), jnp.int32).at[ranking[jnp.where(places < fixed, places, moved)]].set(jnp.asarray(lengths, jnp.int32))

    lengths = jnp.where(number % 4 == 0, named(heavy_load, number // 4), named(common, number - number // 4 - 1))
    mixed = jax.random.permutation(jax.random.fold_in(own, 3), amount)
    giver, receiver = mixed[0:amount // 2 * 2:2], mixed[1:amount // 2 * 2:2]
    margin = jnp.minimum(lengths[giver] - 1, most - lengths[receiver]) // 2
    margin = jnp.where((giver == ranking[0]) | (receiver == ranking[0]) | (lengths[receiver] == 0), 0, jnp.maximum(margin, 0))
    moved = jax.random.randint(jax.random.fold_in(own, 4), (amount // 2,), 0, 1 << 20) % (margin + 1)
    lengths = lengths.at[giver].add(-moved).at[receiver].add(moved)
    items = jnp.searchsorted(jnp.cumsum(lengths), jnp.arange(rows * top), side="right").astype(jnp.int32)
    grid = items.reshape(top, rows).T
    grid = grid[jax.random.permutation(jax.random.fold_in(own, 1), rows)]
    offset_by = jax.random.randint(jax.random.fold_in(own, 2), (rows, 1), 0, top)
    return jnp.take_along_axis(grid, (jnp.arange(top)[None, :] + offset_by) % top, axis=1)


def portions_of(amount, total, reach, slope, full):
    portions = [(1 << 20) // math.isqrt(grade ** slope) + 1 for grade in range(1, amount + 1)]
    largest = reach if full else min(reach, max(-(-total // amount), total * portions[0] // sum(portions)))
    least = 1 if total - largest >= amount - 1 else 0
    holding, rest = [largest] + [least] * (amount - 1), total - largest - least * (amount - 1)
    while rest > 0:
        free = [i for i in range(1, amount) if holding[i] < largest] or [i for i in range(1, amount) if holding[i] < reach]
        pool, remaining = sum([portions[i] for i in free]), rest
        for i in free:
            addition = min(reach - holding[i], max(1, remaining * portions[i] // pool), rest)
            holding[i] = holding[i] + addition
            rest = rest - addition
    return np.array(holding)


def noise(key, dims, width, limit, cuts=(), held_as=jnp.bfloat16):
    values = width * jax.random.normal(key, dims, jnp.float32)
    if cuts:
        values = values * level_of(key, dims, cuts, -0.22, 0.18)
    return jnp.clip(values, -limit, limit).astype(held_as)


def setup_inputs(seed: int = 0) -> dict:
    seeds = jax.random.split(jax.random.key(seed), 8)
    tokens = noise(seeds[0], (MICRO, MB_TOK, D), 1.0, 6.0, ((0, 4), (1, 32)))
    norm_gain = jnp.clip(1.0 + 0.1 * jax.random.normal(seeds[1], (N_SECTION, D), jnp.float32), 0.5, 1.5)
    gate_weight = noise(seeds[2], (N_SECTION, D, EXPERTS * FFE), D ** -0.5, 0.0625, ((0, 4), (2, 32)))
    up_weight = noise(seeds[3], (N_SECTION, D, EXPERTS * FFE), D ** -0.5, 0.0625, ((0, 4), (2, 32)))
    down_weight = noise(seeds[4], (N_SECTION, EXPERTS * FFE, D), FFE ** -0.5, 0.125, ((0, 4), (1, 32)))
    routes_keys = jax.random.split(jax.random.fold_in(seeds[5], 1), N_SECTION * MICRO * MB_TOK // TOK_DEV)
    routes_turns = jax.random.permutation(jax.random.fold_in(seeds[5], 3), N_SECTION * MICRO * MB_TOK // TOK_DEV)
    routes = jax.vmap(lambda own, number: deal_out(jax.random.fold_in(seeds[5], 2), own, number, TOK_DEV, EXPERTS, TOPK, CAP, 2))(routes_keys, routes_turns).reshape((N_SECTION, MICRO, MB_TOK, TOPK))
    route_weights = jnp.clip(0.2 + 1 * jax.random.uniform(seeds[6], (N_SECTION, MICRO, MB_TOK, TOPK), jnp.float32) ** level_of(seeds[6], (N_SECTION, MICRO, MB_TOK, TOPK), ((0, 4), (2, 32)), -0.2, 0.2), 0.2, 1.2)
    return {"tokens": tokens, "norm_gain": norm_gain, "gate_weight": gate_weight, "up_weight": up_weight, "down_weight": down_weight, "routes": routes, "route_weights": route_weights}


def normalize(hidden, gain):
    widened = hidden.astype(jnp.float32)
    scale = lax.rsqrt(lax.optimization_barrier(jnp.mean(widened * widened, axis=-1, keepdims=True)) + 1e-06)
    return (widened * scale * gain).astype(jnp.bfloat16)

def moe_layer(hidden, gain, gate_weight, up_weight, down_weight, route_ids, route_scale):
    normed = normalize(hidden, gain)
    flat_ids = route_ids.reshape(-1).astype(jnp.int32)
    flat_scale = route_scale.reshape(-1)
    bound = N_EXPERT * CAP
    part_width = FFE // SHARDS

    def add_expert(expert, total):
        expert = jnp.asarray(expert).astype(jnp.int32)
        sort_keys = jnp.where(flat_ids == expert, 0, 1).astype(jnp.int32)
        ordering = jnp.argsort(sort_keys, stable=True)[:bound].astype(jnp.int32)
        token_rows = (ordering // TOPK).astype(jnp.int32)
        weights = jnp.where(flat_ids[ordering] == expert, flat_scale[ordering], jnp.zeros_like(flat_scale[ordering]))
        picked = normed[token_rows]
        start = (expert * FFE).astype(jnp.int32)
        gate_cols = lax.dynamic_slice_in_dim(gate_weight, start, FFE, 1)
        up_cols = lax.dynamic_slice_in_dim(up_weight, start, FFE, 1)
        gate_pre = jnp.dot(picked, gate_cols, preferred_element_type=jnp.float32)
        up_pre = jnp.dot(picked, up_cols, preferred_element_type=jnp.float32)
        inner = (jax.nn.silu(gate_pre) * up_pre).astype(jnp.bfloat16)
        down_rows = lax.dynamic_slice_in_dim(down_weight, start, FFE, 0).astype(jnp.float32)
        down_rows = down_rows.reshape(SHARDS, part_width, D)
        partial_value = jnp.einsum('rsh,shd->rsd', inner.astype(jnp.float32).reshape(bound, SHARDS, part_width), down_rows)
        partial_value = lax.optimization_barrier(partial_value.astype(jnp.bfloat16)).astype(jnp.float32)
        term = lax.optimization_barrier(jnp.sum(partial_value, axis=1)) * weights[:, None]
        return total + jax.ops.segment_sum(term, token_rows, num_segments=hidden.shape[0])
    total = lax.fori_loop(0, EXPERTS, add_expert, jnp.zeros(hidden.shape, jnp.float32))
    return (hidden.astype(jnp.float32) + total).astype(jnp.bfloat16)

def reference(tokens, norm_gain, gate_weight, up_weight, down_weight, routes, route_weights):
    results = []
    for batch_index in range(MICRO):
        hidden = tokens[batch_index]
        for layer_index in range(N_SECTION):
            hidden = moe_layer(hidden, norm_gain[layer_index], gate_weight[layer_index], up_weight[layer_index], down_weight[layer_index], routes[layer_index, batch_index], route_weights[layer_index, batch_index])
        results.append(hidden)
    return jnp.stack(results)
```

```python
import jax
import jax.numpy as jnp
from jax import lax
from jax.experimental import pallas as pl
from jax.experimental.pallas import tpu as pltpu
from jax.sharding import PartitionSpec as P

SHARDS = 4
PARTS = 4

F32 = jnp.float32
BF16 = jnp.bfloat16


def params():
    return pltpu.CompilerParams(vmem_limit_bytes=28 * 1024 * 1024)


def cost(flops, bytes_accessed):
    return pl.CostEstimate(flops=int(flops), bytes_accessed=int(bytes_accessed), transcendentals=0)


def mm(a, b):
    return jnp.dot(a, b, preferred_element_type=F32)


def front(pos, hidden, gain, pick, *, width):
    tok, full = hidden.shape
    rows, depth = pick.shape[1:]
    blocks = full // width

    def kernel(pos_ref, h_ref, g_ref, p_ref, o_ref):
        x = h_ref[...].astype(F32)
        scale = lax.rsqrt(jnp.mean(x * x, axis=-1, keepdims=True) + 1e-06)
        normed = (x * scale * g_ref[...]).astype(BF16)
        stack = jnp.concatenate([normed[:, b * width : (b + 1) * width] for b in range(blocks)], axis=0)
        o_ref[...] = mm(p_ref[0], stack).astype(BF16)

    return pl.pallas_call(
        kernel,
        out_shape=jax.ShapeDtypeStruct((rows, width), BF16),
        grid_spec=pltpu.PrefetchScalarGridSpec(
            num_scalar_prefetch=1,
            grid=(1,),
            in_specs=[
                pl.BlockSpec((tok, full), lambda i, s: (0, 0)),
                pl.BlockSpec((1, full), lambda i, s: (0, 0)),
                pl.BlockSpec((1, rows, depth), lambda i, s: (s[0], 0, 0)),
            ],
            out_specs=pl.BlockSpec((rows, width), lambda i, s: (0, 0)),
        ),
        compiler_params=params(),
        cost_estimate=cost(2 * rows * depth * width, 2 * rows * width),
    )(pos, hidden, gain, pick)


def unpack(packed_ref, perm, xs, slot_rows):
    group = perm.shape[0]
    piece = group // PARTS
    for g in range(slot_rows // piece):
        moved = mm(perm, packed_ref[g * group : (g + 1) * group, :]).astype(BF16)
        for b in range(PARTS):
            xs[b, g * piece : (g + 1) * piece, :] = moved[b * piece : (b + 1) * piece]


def repack(ys, perm, g):
    group = perm.shape[0]
    piece = group // PARTS
    stack = jnp.concatenate([ys[b, g * piece : (g + 1) * piece, :] for b in range(PARTS)], axis=0)
    return mm(perm, stack)


def first_half(core, arrived, perm, gate, up):
    all_rows, width = arrived.shape
    rows = all_rows // PARTS
    units = gate.shape[2]

    def kernel(core_ref, a_ref, p_ref, g_ref, u_ref, og_ref, ou_ref, xs):
        step = pl.program_id(0)

        @pl.when(step == 0)
        def _():
            unpack(a_ref, p_ref[...], xs, rows)
            og_ref[...] = jnp.zeros_like(og_ref)
            ou_ref[...] = jnp.zeros_like(ou_ref)

        x = xs[step]
        og_ref[...] += mm(x, g_ref[0])
        ou_ref[...] += mm(x, u_ref[0])

    weight = pl.BlockSpec((1, width, units), lambda i, s: (0, s[0] * PARTS + i, 0))
    total = pl.BlockSpec((rows, units), lambda i, s: (0, 0))
    return pl.pallas_call(
        kernel,
        out_shape=[jax.ShapeDtypeStruct((rows, units), F32)] * 2,
        grid_spec=pltpu.PrefetchScalarGridSpec(
            num_scalar_prefetch=1,
            grid=(PARTS,),
            in_specs=[
                pl.BlockSpec((all_rows, width), lambda i, s: (0, 0)),
                pl.BlockSpec(perm.shape, lambda i, s: (0, 0)),
                weight,
                weight,
            ],
            out_specs=[total, total],
            scratch_shapes=[pltpu.VMEM((PARTS, rows, width), BF16)],
        ),
        compiler_params=params(),
        cost_estimate=cost(4 * all_rows * width * units, 4 * PARTS * width * units),
    )(core, arrived, perm, gate, up)


def second_half(core, arrived, perm, back, gate, up, down, sum_gate, sum_up):
    all_rows, width = arrived.shape
    rows = all_rows // PARTS
    units = gate.shape[2]

    def kernel(core_ref, a_ref, p_ref, q_ref, g_ref, u_ref, d_ref, sg_ref, su_ref, o_ref, i_ref, xs, tg, tu):
        step = pl.program_id(0)

        @pl.when(step == 0)
        def _():
            unpack(a_ref, p_ref[...], xs, rows)
            tg[...] = sg_ref[...]
            tu[...] = su_ref[...]

        @pl.when(step < PARTS)
        def _():
            x = xs[step]
            tg[...] += mm(x, g_ref[0])
            tu[...] += mm(x, u_ref[0])

        @pl.when(step == PARTS - 1)
        def _():
            pre = tg[...]
            i_ref[...] = (pre * lax.logistic(pre) * tu[...]).astype(BF16)

        @pl.when(step >= PARTS)
        def _():
            xs[step - PARTS] = mm(i_ref[...], d_ref[0]).astype(BF16)

        @pl.when(step == 2 * PARTS - 1)
        def _():
            group = perm.shape[0]
            for g in range(all_rows // group):
                o_ref[g * group : (g + 1) * group, :] = repack(xs, q_ref[...], g).astype(BF16)

    last = PARTS - 1
    weight = pl.BlockSpec(
        (1, width, units), lambda i, s: (0, (1 - s[0]) * PARTS + jnp.minimum(i, last), 0)
    )
    lower = pl.BlockSpec(
        (1, units, width), lambda i, s: (0, 0, (1 - s[0]) * PARTS + jnp.maximum(i - PARTS, 0))
    )
    whole = lambda i, s: (0, 0)
    return pl.pallas_call(
        kernel,
        out_shape=[
            jax.ShapeDtypeStruct((all_rows, width), BF16),
            jax.ShapeDtypeStruct((rows, units), BF16),
        ],
        grid_spec=pltpu.PrefetchScalarGridSpec(
            num_scalar_prefetch=1,
            grid=(2 * PARTS,),
            in_specs=[
                pl.BlockSpec((all_rows, width), whole),
                pl.BlockSpec(perm.shape, whole),
                pl.BlockSpec(perm.shape, whole),
                weight,
                weight,
                lower,
                pl.BlockSpec((rows, units), whole),
                pl.BlockSpec((rows, units), whole),
            ],
            out_specs=[pl.BlockSpec((all_rows, width), whole), pl.BlockSpec((rows, units), whole)],
            scratch_shapes=[
                pltpu.VMEM((PARTS, rows, width), BF16),
                pltpu.VMEM((rows, units), F32),
                pltpu.VMEM((rows, units), F32),
            ],
        ),
        compiler_params=params(),
        cost_estimate=cost(6 * all_rows * width * units, 6 * PARTS * width * units),
    )(core, arrived, perm, back, gate, up, down, sum_gate, sum_up)


def own_down(core, inner, down, received, back):
    all_rows, width = received.shape
    rows, units = inner.shape

    def kernel(core_ref, i_ref, d_ref, r_ref, q_ref, o_ref, ys):
        step = pl.program_id(0)
        ys[step] = mm(i_ref[...], d_ref[0]).astype(BF16)

        @pl.when(step == PARTS - 1)
        def _():
            group = back.shape[0]
            for g in range(all_rows // group):
                part = slice(g * group, (g + 1) * group)
                o_ref[part, :] = (repack(ys, q_ref[...], g) + r_ref[part, :].astype(F32)).astype(BF16)

    whole = lambda i, s: (0, 0)
    return pl.pallas_call(
        kernel,
        out_shape=jax.ShapeDtypeStruct((all_rows, width), BF16),
        grid_spec=pltpu.PrefetchScalarGridSpec(
            num_scalar_prefetch=1,
            grid=(PARTS,),
            in_specs=[
                pl.BlockSpec((rows, units), whole),
                pl.BlockSpec((1, units, width), lambda i, s: (0, 0, s[0] * PARTS + i)),
                pl.BlockSpec((all_rows, width), whole),
                pl.BlockSpec(back.shape, whole),
            ],
            out_specs=pl.BlockSpec((all_rows, width), whole),
            scratch_shapes=[pltpu.VMEM((PARTS, rows, width), BF16)],
        ),
        compiler_params=params(),
        cost_estimate=cost(2 * all_rows * width * units, 2 * PARTS * width * units),
    )(core, inner, down, received, back)


def combine(flags, returned, spread, scales, hidden, tokens):
    rows, width = returned.shape
    tok, full = hidden.shape
    blocks = full // width
    picks = spread.shape[1] // blocks
    routes_each = picks // tok

    def kernel(f_ref, r_ref, s_ref, w_ref, h_ref, t_ref, o_ref):
        got = mm(s_ref[0], r_ref[...])
        live = f_ref[1] == 1
        for b in range(blocks):
            cols = slice(b * width, (b + 1) * width)
            total = h_ref[:, cols].astype(F32)
            for k in range(routes_each):
                at = b * picks + k * tok
                total += w_ref[0, k * tok : (k + 1) * tok, :] * got[at : at + tok]
            o_ref[:, cols] = jnp.where(live, total, t_ref[:, cols].astype(F32)).astype(BF16)

    whole = lambda i, s: (0, 0)
    return pl.pallas_call(
        kernel,
        out_shape=jax.ShapeDtypeStruct((tok, full), BF16),
        grid_spec=pltpu.PrefetchScalarGridSpec(
            num_scalar_prefetch=1,
            grid=(1,),
            in_specs=[
                pl.BlockSpec((rows, width), whole),
                pl.BlockSpec((1,) + spread.shape[1:], lambda i, s: (s[0], 0, 0)),
                pl.BlockSpec((1, picks, 1), lambda i, s: (s[0], 0, 0)),
                pl.BlockSpec((tok, full), whole),
                pl.BlockSpec((tok, full), whole),
            ],
            out_specs=pl.BlockSpec((tok, full), whole),
        ),
        compiler_params=params(),
        cost_estimate=cost(2 * spread.shape[1] * rows * width, 2 * rows * width),
    )(flags, returned, spread, scales, hidden, tokens)


def per_device(tokens, norm_gain, gate_weight, up_weight, down_weight, routes, route_weights):
    sections = lax.axis_size("section")
    devices = lax.axis_size("expert")
    experts = devices // SHARDS
    _, batches, tok, routes_each = routes.shape
    full = tokens.shape[2]
    capacity = min(tok, tok * routes_each * 3 // (2 * experts))
    width = full // (2 * PARTS)
    section = lax.axis_index("section")
    core = lax.rem(lax.axis_index("expert"), 2).astype(jnp.int32).reshape(1)
    own = tokens[0]

    ids = routes[0].reshape(batches, tok * routes_each)
    order = jnp.arange(tok * routes_each)
    same = (ids[:, :, None] == ids[:, None, :]) & (order[None, :] < order[:, None])
    code = (ids * capacity + jnp.sum(same.astype(jnp.int32), axis=2)).reshape(batches, tok, routes_each)
    row = jnp.arange(devices * PARTS * capacity, dtype=jnp.int32)
    device = row // (PARTS * capacity)
    row_block = (device % 2) * PARTS + (row % (PARTS * capacity)) // capacity
    row_slot = (device // SHARDS) * capacity + row % capacity
    blocks = jnp.arange(2 * PARTS, dtype=jnp.int32)
    code = jnp.moveaxis(code, 2, 1)
    hits = (code[:, None, :, :, None] == row_slot) & (blocks[:, None, None, None] == row_block)
    spread = hits.reshape(batches, -1, row.shape[0]).astype(BF16)
    hits_t = (row_slot[:, None, None, None] == code[:, None, :, None, :]) & (
        row_block[:, None, None, None] == blocks[:, None]
    )
    pick = jnp.any(hits_t, axis=2).reshape(batches, row.shape[0], -1).astype(BF16)
    scales = jnp.moveaxis(route_weights[0], 2, 1).reshape(batches, tok * routes_each, 1)

    group = 8 * PARTS * capacity
    at = jnp.arange(group, dtype=jnp.int32)
    wanted = (at % (8 * capacity)) // capacity * (PARTS * capacity) + at // (8 * capacity) * capacity + at % capacity
    perm = (wanted[:, None] == at[None, :]).astype(BF16)
    back = (at[:, None] == wanted[None, :]).astype(BF16)

    swap = [(i, i ^ 1) for i in range(devices)]
    hidden = own
    kept = None
    for step in range(batches + sections - 1):
        if step > 0:
            begins = max(0, step - batches)
            pairs = [(i, i + 1) for i in range(begins, min(step, sections - 1))]
            if step < batches:
                pairs.append((step, 0))
            else:
                pairs.append((sections - 1, step - batches))
            hidden = lax.ppermute(current, "section", pairs)
            if step >= batches:
                home = step - batches
                kept = hidden if kept is None else jnp.where(section == home, hidden, kept)
        batch = step - section
        pos = jnp.clip(batch, 0, batches - 1).astype(jnp.int32)
        flags = jnp.stack([pos, (batch >= 0).astype(jnp.int32)])
        packed = front(pos.reshape(1), hidden, norm_gain, pick, width=width)
        arrived = lax.all_to_all(packed, "expert", split_axis=0, concat_axis=0, tiled=True)
        others = lax.ppermute(arrived, "expert", swap)
        sum_gate, sum_up = first_half(core, arrived, perm, gate_weight, up_weight)
        leaving, inner = second_half(
            core, others, perm, back, gate_weight, up_weight, down_weight, sum_gate, sum_up
        )
        received = lax.ppermute(leaving, "expert", swap)
        partial_value = own_down(core, inner, down_weight, received, back)
        returned = lax.all_to_all(partial_value, "expert", split_axis=0, concat_axis=0, tiled=True)
        current = combine(flags, returned, spread, scales, hidden, own)
    return jnp.where(section == sections - 1, current, kept)[None]


def solution(mesh):
    return jax.shard_map(
        per_device,
        mesh=mesh,
        in_specs=(
            P("section", "expert", None),
            P("section", None),
            P("section", None, "expert"),
            P("section", None, "expert"),
            P("section", "expert", None),
            P("section", None, "expert", None),
            P("section", None, "expert", None),
        ),
        out_specs=P("section", "expert", None),
        check_vma=False,
    )
```

```python
import jax
import jax.numpy as jnp
from jax import lax
from jax.experimental import pallas as pl
from jax.experimental.pallas import tpu as pltpu
from jax.sharding import PartitionSpec as P

SHARDS = 4
PARTS = 4

F32 = jnp.float32
BF16 = jnp.bfloat16


def params():
    return pltpu.CompilerParams(vmem_limit_bytes=12 * 1024 * 1024)


def cost(flops, bytes_accessed):
    return pl.CostEstimate(flops=int(flops), bytes_accessed=int(bytes_accessed), transcendentals=0)


def mm(a, b):
    return jnp.dot(a, b, preferred_element_type=F32)


def batch_at(step, place, batches):
    return jnp.clip(step - place[0], 0, batches - 1)


def front(place, hidden, gain, pick, step, *, width):
    tok, full = hidden.shape
    batches, rows, depth = pick.shape
    blocks = full // width

    def kernel(place_ref, h_ref, g_ref, p_ref, o_ref):
        x = h_ref[...].astype(F32)
        scale = lax.rsqrt(jnp.mean(x * x, axis=-1, keepdims=True) + 1e-06)
        normed = (x * scale * g_ref[...]).astype(BF16)
        stack = jnp.concatenate([normed[:, b * width : (b + 1) * width] for b in range(blocks)], axis=0)
        o_ref[...] = mm(p_ref[0], stack).astype(BF16)

    return pl.pallas_call(
        kernel,
        out_shape=jax.ShapeDtypeStruct((rows, width), BF16),
        grid_spec=pltpu.PrefetchScalarGridSpec(
            num_scalar_prefetch=1,
            grid=(1,),
            in_specs=[
                pl.BlockSpec((tok, full), lambda i, s: (0, 0)),
                pl.BlockSpec((1, full), lambda i, s: (0, 0)),
                pl.BlockSpec((1, rows, depth), lambda i, s: (batch_at(step, s, batches), 0, 0)),
            ],
            out_specs=pl.BlockSpec((rows, width), lambda i, s: (0, 0)),
        ),
        compiler_params=params(),
        cost_estimate=cost(2 * rows * depth * width, 2 * rows * width),
    )(place, hidden, gain, pick)


def stage(weights):
    def kernel(*refs):
        count = len(weights)
        sems = refs[-1]
        copies = [
            pltpu.make_async_copy(refs[i], refs[count + i], sems.at[i]) for i in range(count)
        ]
        for copy in copies:
            copy.start()
        for copy in copies:
            copy.wait()

    staged = pl.pallas_call(
        kernel,
        out_shape=[pltpu.VMEM(w.shape, w.dtype) for w in weights],
        in_specs=[pl.BlockSpec(memory_space=pltpu.HBM)] * len(weights),
        out_specs=[pl.BlockSpec(memory_space=pltpu.VMEM)] * len(weights),
        scratch_shapes=[pltpu.SemaphoreType.DMA((len(weights),))],
        compiler_params=params(),
        cost_estimate=cost(0, 2 * sum(w.size * 2 for w in weights)),
    )(*[pltpu.with_memory_space_constraint(w, pltpu.HBM) for w in weights])
    return staged


def held(array):
    return pltpu.with_memory_space_constraint(array, pltpu.VMEM)


def unpack(packed_ref, perm, xs, rows):
    group, width = perm.shape[0], packed_ref.shape[1]
    piece = group // PARTS
    for g in range(rows // piece):
        moved = mm(perm, packed_ref[g * group : (g + 1) * group, :]).astype(BF16)
        for b in range(PARTS):
            xs[g * piece : (g + 1) * piece, b * width : (b + 1) * width] = moved[b * piece : (b + 1) * piece]


def down_packed(inner, down_ref, half, perm, ys, out_ref):
    group, width = perm.shape[0], out_ref.shape[1]
    piece = group // PARTS
    for b in range(PARTS):
        cols = pl.ds(pl.multiple_of(half * (PARTS * width) + b * width, 128), width)
        ys[b] = mm(inner, down_ref[0, :, cols]).astype(BF16)
    for g in range(out_ref.shape[0] // group):
        stack = jnp.concatenate([ys[b, g * piece : (g + 1) * piece, :] for b in range(PARTS)], axis=0)
        out_ref[g * group : (g + 1) * group, :] = mm(perm, stack).astype(BF16)


SMEM_IN = pl.BlockSpec(memory_space=pltpu.SMEM)
VMEM_IN = pl.BlockSpec(memory_space=pltpu.VMEM)


def first_half(place, arrived, perm, gate, up):
    all_rows, width = arrived.shape
    rows = all_rows // PARTS
    units = gate.shape[2]

    def kernel(place_ref, a_ref, p_ref, g_ref, u_ref, og_ref, ou_ref, xs):
        unpack(a_ref, p_ref[...], xs, rows)
        depth = PARTS * width
        part = pl.ds(pl.multiple_of(place_ref[1] * depth, depth), depth)
        og_ref[...] = mm(xs[...], g_ref[0, part, :])
        ou_ref[...] = mm(xs[...], u_ref[0, part, :])

    return pl.pallas_call(
        kernel,
        out_shape=[jax.ShapeDtypeStruct((rows, units), F32)] * 2,
        in_specs=[SMEM_IN] + [VMEM_IN] * 4,
        out_specs=[VMEM_IN] * 2,
        scratch_shapes=[pltpu.VMEM((rows, PARTS * width), BF16)],
        compiler_params=params(),
        cost_estimate=cost(4 * all_rows * width * units, 4 * PARTS * width * units),
    )(place, arrived, perm, held(gate), held(up))


def second_half(place, arrived, perm, back, gate, up, down, sum_gate, sum_up):
    all_rows, width = arrived.shape
    rows = all_rows // PARTS
    units = gate.shape[2]

    def kernel(place_ref, a_ref, p_ref, q_ref, g_ref, u_ref, d_ref, sg_ref, su_ref, o_ref, i_ref, xs, ys):
        unpack(a_ref, p_ref[...], xs, rows)
        depth = PARTS * width
        other = 1 - place_ref[1]
        part = pl.ds(pl.multiple_of(other * depth, depth), depth)
        pre = sg_ref[...] + mm(xs[...], g_ref[0, part, :])
        upper = su_ref[...] + mm(xs[...], u_ref[0, part, :])
        i_ref[...] = (pre * lax.logistic(pre) * upper).astype(BF16)
        down_packed(i_ref[...], d_ref, other, q_ref[...], ys, o_ref)

    return pl.pallas_call(
        kernel,
        out_shape=[
            jax.ShapeDtypeStruct((all_rows, width), BF16),
            jax.ShapeDtypeStruct((rows, units), BF16),
        ],
        in_specs=[SMEM_IN] + [VMEM_IN] * 8,
        out_specs=[VMEM_IN] * 2,
        scratch_shapes=[
            pltpu.VMEM((rows, PARTS * width), BF16),
            pltpu.VMEM((PARTS, rows, width), BF16),
        ],
        compiler_params=params(),
        cost_estimate=cost(6 * all_rows * width * units, 6 * PARTS * width * units),
    )(place, arrived, perm, back, held(gate), held(up), held(down), sum_gate, sum_up)


def own_down(place, inner, down, back):
    rows, units = inner.shape
    width = down.shape[2] // (2 * PARTS)

    def kernel(place_ref, i_ref, d_ref, q_ref, o_ref, ys):
        down_packed(i_ref[...], d_ref, place_ref[1], q_ref[...], ys, o_ref)

    return pl.pallas_call(
        kernel,
        out_shape=jax.ShapeDtypeStruct((rows * PARTS, width), BF16),
        in_specs=[SMEM_IN] + [VMEM_IN] * 3,
        out_specs=VMEM_IN,
        scratch_shapes=[pltpu.VMEM((PARTS, rows, width), BF16)],
        compiler_params=params(),
        cost_estimate=cost(2 * rows * PARTS * width * units, 2 * PARTS * width * units),
    )(place, inner, held(down), back)


def combine(place, returned, spread, scales, hidden, tokens, step, finished=()):
    rows, width = returned.shape
    tok, full = hidden.shape
    batches = spread.shape[0]
    blocks = full // width
    picks = spread.shape[1] // blocks
    routes_each = picks // tok

    def kernel(place_ref, r_ref, s_ref, w_ref, h_ref, t_ref, *rest):
        o_ref = rest[-1]
        got = mm(s_ref[0], r_ref[...])
        section = place_ref[0]
        for b in range(blocks):
            cols = slice(b * width, (b + 1) * width)
            total = h_ref[:, cols].astype(F32)
            for k in range(routes_each):
                at = b * picks + k * tok
                total += w_ref[0, k * tok : (k + 1) * tok, :1] * got[at : at + tok]
            total = jnp.where(section <= step, total, t_ref[:, cols].astype(F32))
            for home, f_ref in enumerate(rest[:-1]):
                total = jnp.where(section == home, f_ref[:, cols].astype(F32), total)
            o_ref[:, cols] = total.astype(BF16)

    whole = lambda i, s: (0, 0)
    chosen = lambda i, s: (batch_at(step, s, batches), 0, 0)
    return pl.pallas_call(
        kernel,
        out_shape=jax.ShapeDtypeStruct((tok, full), BF16),
        grid_spec=pltpu.PrefetchScalarGridSpec(
            num_scalar_prefetch=1,
            grid=(1,),
            in_specs=[
                pl.BlockSpec((rows, width), whole),
                pl.BlockSpec((1,) + spread.shape[1:], chosen),
                pl.BlockSpec((1, picks, 128), chosen),
            ]
            + [pl.BlockSpec((tok, full), whole)] * (2 + len(finished)),
            out_specs=pl.BlockSpec((tok, full), whole),
        ),
        compiler_params=params(),
        cost_estimate=cost(2 * spread.shape[1] * rows * width, 2 * rows * width),
    )(place, returned, spread, scales, hidden, tokens, *finished)


def per_device(tokens, norm_gain, gate_weight, up_weight, down_weight, routes, route_weights):
    sections = lax.axis_size("section")
    devices = lax.axis_size("expert")
    experts = devices // SHARDS
    _, batches, tok, routes_each = routes.shape
    full = tokens.shape[2]
    capacity = min(tok, tok * routes_each * 3 // (2 * experts))
    width = full // (2 * PARTS)
    section = lax.axis_index("section")
    core = lax.axis_index("expert") % 2
    place = jnp.stack([section, core]).astype(jnp.int32)
    own = tokens[0]

    ids = routes[0].reshape(batches, tok * routes_each)
    order = jnp.arange(tok * routes_each)
    same = (ids[:, :, None] == ids[:, None, :]) & (order[None, :] < order[:, None])
    code = (ids * capacity + jnp.sum(same.astype(jnp.int32), axis=2)).reshape(batches, tok, routes_each)
    row = jnp.arange(devices * PARTS * capacity, dtype=jnp.int32)
    device = row // (PARTS * capacity)
    row_block = (device % 2) * PARTS + (row % (PARTS * capacity)) // capacity
    row_slot = (device // SHARDS) * capacity + row % capacity
    blocks = jnp.arange(2 * PARTS, dtype=jnp.int32)
    code = jnp.moveaxis(code, 2, 1)
    hits = (code[:, None, :, :, None] == row_slot) & (blocks[:, None, None, None] == row_block)
    spread = hits.reshape(batches, -1, row.shape[0]).astype(BF16)
    hits_t = (row_slot[:, None, None, None] == code[:, None, :, None, :]) & (
        row_block[:, None, None, None] == blocks[:, None]
    )
    pick = jnp.any(hits_t, axis=2).reshape(batches, row.shape[0], -1).astype(BF16)
    scales = jnp.moveaxis(route_weights[0], 2, 1).reshape(batches, tok * routes_each, 1)
    scales = jnp.broadcast_to(scales, scales.shape[:2] + (128,))

    group = 8 * PARTS * capacity
    at = jnp.arange(group, dtype=jnp.int32)
    wanted = (at % (8 * capacity)) // capacity * (PARTS * capacity) + at // (8 * capacity) * capacity + at % capacity
    perm = (wanted[:, None] == at[None, :]).astype(BF16)
    back = (at[:, None] == wanted[None, :]).astype(BF16)

    swap = [(i, i ^ 1) for i in range(devices)]
    place, pick, spread, scales, perm, back = lax.optimization_barrier((place, pick, spread, scales, perm, back))
    gate, up, down = stage([gate_weight, up_weight, down_weight])
    hidden = own
    finished = []
    for step in range(batches + sections - 1):
        if step > 0:
            begins = max(0, step - batches)
            pairs = [(i, i + 1) for i in range(begins, min(step, sections - 1))]
            if step < batches:
                pairs.append((step, 0))
            else:
                pairs.append((sections - 1, step - batches))
            hidden = lax.ppermute(current, "section", pairs)
            if step >= batches:
                finished.append(hidden)
        packed = front(place, hidden, norm_gain, pick, step, width=width)
        arrived = lax.all_to_all(packed, "expert", split_axis=0, concat_axis=0, tiled=True)
        others = lax.ppermute(arrived, "expert", swap)
        sum_gate, sum_up = first_half(place, arrived, perm, gate, up)
        leaving, inner = second_half(place, others, perm, back, gate, up, down, sum_gate, sum_up)
        received = lax.ppermute(leaving, "expert", swap)
        staying = own_down(place, inner, down, back)
        partial_value = (staying.astype(F32) + received.astype(F32)).astype(BF16)
        returned = lax.all_to_all(partial_value, "expert", split_axis=0, concat_axis=0, tiled=True)
        is_last = step == batches + sections - 2
        current = combine(
            place, returned, spread, scales, hidden, own, step, finished if is_last else ()
        )
    return current[None]


def solution(mesh):
    return jax.shard_map(
        per_device,
        mesh=mesh,
        in_specs=(
            P("section", "expert", None),
            P("section", None),
            P("section", None, "expert"),
            P("section", None, "expert"),
            P("section", "expert", None),
            P("section", None, "expert", None),
            P("section", None, "expert", None),
        ),
        out_specs=P("section", "expert", None),
        check_vma=False,
    )
```

```python
import jax
import jax.numpy as jnp
import numpy as np
from jax import lax
from jax.experimental import pallas as pl
from jax.experimental.pallas import tpu as pltpu
from jax.sharding import PartitionSpec as P

SHARDS = 4
PARTS = 4

F32 = jnp.float32
BF16 = jnp.bfloat16


def params():
    return pltpu.CompilerParams(vmem_limit_bytes=12 * 1024 * 1024)


def cost(flops, bytes_accessed):
    return pl.CostEstimate(flops=int(flops), bytes_accessed=int(bytes_accessed), transcendentals=0)


def mm(a, b):
    return jnp.dot(a, b, preferred_element_type=F32)


def batch_at(step, place, batches):
    return jnp.clip(step - place[0], 0, batches - 1)


def front(place, hidden, gain, keys, row_keys, step, *, width, experts):
    tok, full = hidden.shape
    batches, routes_each, lanes = keys.shape
    rows = row_keys.shape[0]
    blocks = full // width
    piece = rows // experts

    def kernel(place_ref, h_ref, g_ref, k_ref, r_ref, o_ref):
        x = h_ref[...].astype(F32)
        scale = lax.rsqrt(jnp.mean(x * x, axis=-1, keepdims=True) + 1e-06)
        normed = (x * scale * g_ref[...]).astype(BF16)
        stack = jnp.concatenate([normed[:, b * width : (b + 1) * width] for b in range(blocks)], axis=0)
        hit = r_ref[...] == k_ref[0, :1, :]
        for k in range(1, routes_each):
            hit |= r_ref[...] == k_ref[0, k : k + 1, :]
        out = mm(jnp.where(hit, 1.0, 0.0).astype(BF16), stack).astype(BF16)
        for e in range(experts):
            for chip in range(2):
                at = (2 * e + chip) * piece
                o_ref[at : at + piece, :] = out[e * piece : (e + 1) * piece]

    return pl.pallas_call(
        kernel,
        out_shape=jax.ShapeDtypeStruct((2 * rows, width), BF16),
        grid_spec=pltpu.PrefetchScalarGridSpec(
            num_scalar_prefetch=1,
            grid=(1,),
            in_specs=[
                pl.BlockSpec((tok, full), lambda i, s: (0, 0)),
                pl.BlockSpec((1, full), lambda i, s: (0, 0)),
                pl.BlockSpec((1, routes_each, lanes), lambda i, s: (batch_at(step, s, batches), 0, 0)),
                pl.BlockSpec((rows, lanes), lambda i, s: (0, 0)),
            ],
            out_specs=pl.BlockSpec((2 * rows, width), lambda i, s: (0, 0)),
        ),
        compiler_params=params(),
        cost_estimate=cost(2 * rows * lanes * width, 4 * rows * width),
    )(place, hidden, gain, keys, row_keys)


def held(array):
    return pltpu.with_memory_space_constraint(array, pltpu.VMEM)


def unpack(packed_ref, perm, xs, rows):
    group, width = perm.shape[0], packed_ref.shape[1]
    piece = group // PARTS
    for g in range(rows // piece):
        moved = mm(perm, packed_ref[g * group : (g + 1) * group, :]).astype(BF16)
        for b in range(PARTS):
            xs[g * piece : (g + 1) * piece, b * width : (b + 1) * width] = moved[b * piece : (b + 1) * piece]


def down_packed(inner, down_ref, half, perm, ys, out_ref):
    group, width = perm.shape[0], out_ref.shape[1]
    piece = group // PARTS
    for b in range(PARTS):
        cols = pl.ds(pl.multiple_of(half * (PARTS * width) + b * width, 128), width)
        ys[b] = mm(inner, down_ref[0, :, cols]).astype(BF16)
    for g in range(out_ref.shape[0] // group):
        stack = jnp.concatenate([ys[b, g * piece : (g + 1) * piece, :] for b in range(PARTS)], axis=0)
        out_ref[g * group : (g + 1) * group, :] = mm(perm, stack).astype(BF16)


SMEM_IN = pl.BlockSpec(memory_space=pltpu.SMEM)
VMEM_IN = pl.BlockSpec(memory_space=pltpu.VMEM)


def halves(core, depth):
    own = pl.ds(pl.multiple_of(core * depth, depth), depth)
    other = pl.ds(pl.multiple_of((1 - core) * depth, depth), depth)
    return own, other


def in_hbm(array):
    return pltpu.with_memory_space_constraint(array, pltpu.HBM)


HBM_IN = pl.BlockSpec(memory_space=pltpu.HBM)


def first_half(place, arrived, perm, gate, up, stage):
    all_rows, width = arrived.shape
    rows = all_rows // PARTS
    units = gate.shape[2]
    depth = PARTS * width

    def product(core, xs, g_ref, u_ref, og_ref, ou_ref):
        own, _ = halves(core, depth)
        og_ref[...] = mm(xs[...], g_ref[0, own, :])
        ou_ref[...] = mm(xs[...], u_ref[0, own, :])

    def kernel(place_ref, a_ref, p_ref, g_ref, u_ref, og_ref, ou_ref, xs):
        unpack(a_ref, p_ref[...], xs, rows)
        product(place_ref[1], xs, g_ref, u_ref, og_ref, ou_ref)

    def staging(place_ref, a_ref, p_ref, g_hbm, u_hbm, og_ref, ou_ref, g_ref, u_ref, xs, sems):
        core = place_ref[1]
        copies = []
        for part in halves(core, depth):
            for source, target in ((g_hbm, g_ref), (u_hbm, u_ref)):
                copy = pltpu.make_async_copy(source.at[0, part, :], target.at[0, part, :], sems.at[len(copies)])
                copy.start()
                copies.append(copy)
        unpack(a_ref, p_ref[...], xs, rows)
        copies[0].wait()
        copies[1].wait()
        product(core, xs, g_ref, u_ref, og_ref, ou_ref)
        copies[2].wait()
        copies[3].wait()

    sums = [jax.ShapeDtypeStruct((rows, units), F32)] * 2
    scratch = [pltpu.VMEM((rows, depth), BF16)]
    flops = 4 * all_rows * width * units
    if stage:
        return pl.pallas_call(
            staging,
            out_shape=sums + [pltpu.VMEM(gate.shape, BF16)] * 2,
            in_specs=[SMEM_IN] + [VMEM_IN] * 2 + [HBM_IN] * 2,
            out_specs=[VMEM_IN] * 4,
            scratch_shapes=scratch + [pltpu.SemaphoreType.DMA((4,))],
            compiler_params=params(),
            cost_estimate=cost(flops, 8 * gate.size),
        )(place, arrived, perm, in_hbm(gate), in_hbm(up))
    return pl.pallas_call(
        kernel,
        out_shape=sums,
        in_specs=[SMEM_IN] + [VMEM_IN] * 4,
        out_specs=[VMEM_IN] * 2,
        scratch_shapes=scratch,
        compiler_params=params(),
        cost_estimate=cost(flops, 2 * gate.size),
    )(place, arrived, perm, held(gate), held(up)) + (gate, up)


def second_half(place, arrived, perm, back, gate, up, down, sum_gate, sum_up, stage):
    all_rows, width = arrived.shape
    rows = all_rows // PARTS
    units = gate.shape[2]
    depth = PARTS * width

    def hidden_units(core, a_ref, p_ref, g_ref, u_ref, sg_ref, su_ref, i_ref, xs):
        unpack(a_ref, p_ref[...], xs, rows)
        _, other = halves(core, depth)
        pre = sg_ref[...] + mm(xs[...], g_ref[0, other, :])
        upper = su_ref[...] + mm(xs[...], u_ref[0, other, :])
        i_ref[...] = (pre * lax.logistic(pre) * upper).astype(BF16)

    def kernel(place_ref, a_ref, p_ref, q_ref, g_ref, u_ref, sg_ref, su_ref, d_ref, o_ref, i_ref, xs, ys):
        core = place_ref[1]
        hidden_units(core, a_ref, p_ref, g_ref, u_ref, sg_ref, su_ref, i_ref, xs)
        down_packed(i_ref[...], d_ref, 1 - core, q_ref[...], ys, o_ref)

    def staging(
        place_ref, a_ref, p_ref, q_ref, g_ref, u_ref, sg_ref, su_ref, d_hbm, o_ref, i_ref, d_ref, xs, ys, sem
    ):
        core = place_ref[1]
        copy = pltpu.make_async_copy(d_hbm, d_ref, sem)
        copy.start()
        hidden_units(core, a_ref, p_ref, g_ref, u_ref, sg_ref, su_ref, i_ref, xs)
        copy.wait()
        down_packed(i_ref[...], d_ref, 1 - core, q_ref[...], ys, o_ref)

    outs = [
        jax.ShapeDtypeStruct((all_rows, width), BF16),
        jax.ShapeDtypeStruct((rows, units), BF16),
    ]
    scratch = [pltpu.VMEM((rows, depth), BF16), pltpu.VMEM((PARTS, rows, width), BF16)]
    estimate = cost(6 * all_rows * width * units, 3 * gate.size)
    operands = (place, arrived, perm, back, held(gate), held(up), sum_gate, sum_up)
    if stage:
        return pl.pallas_call(
            staging,
            out_shape=outs + [pltpu.VMEM(down.shape, BF16)],
            in_specs=[SMEM_IN] + [VMEM_IN] * 7 + [HBM_IN],
            out_specs=[VMEM_IN] * 3,
            scratch_shapes=scratch + [pltpu.SemaphoreType.DMA],
            compiler_params=params(),
            cost_estimate=estimate,
        )(*operands, in_hbm(down))
    return pl.pallas_call(
        kernel,
        out_shape=outs,
        in_specs=[SMEM_IN] + [VMEM_IN] * 8,
        out_specs=[VMEM_IN] * 2,
        scratch_shapes=scratch,
        compiler_params=params(),
        cost_estimate=estimate,
    )(*operands, held(down)) + (down,)


def own_down(place, inner, down, back):
    rows, units = inner.shape
    width = down.shape[2] // (2 * PARTS)

    def kernel(place_ref, i_ref, d_ref, q_ref, o_ref, ys):
        down_packed(i_ref[...], d_ref, place_ref[1], q_ref[...], ys, o_ref)

    return pl.pallas_call(
        kernel,
        out_shape=jax.ShapeDtypeStruct((rows * PARTS, width), BF16),
        in_specs=[SMEM_IN] + [VMEM_IN] * 3,
        out_specs=VMEM_IN,
        scratch_shapes=[pltpu.VMEM((PARTS, rows, width), BF16)],
        compiler_params=params(),
        cost_estimate=cost(2 * rows * PARTS * width * units, 2 * PARTS * width * units),
    )(place, inner, held(down), back)


def combine(place, returned, spread, scales, hidden, tokens, step, finished=()):
    rows, width = returned.shape
    tok, full = hidden.shape
    batches = spread.shape[0]
    blocks = full // width
    picks = spread.shape[1] // blocks
    routes_each = picks // tok

    def kernel(place_ref, r_ref, s_ref, w_ref, h_ref, t_ref, *rest):
        o_ref = rest[-1]
        got = mm(s_ref[0], r_ref[...])
        section = place_ref[0]
        for b in range(blocks):
            cols = slice(b * width, (b + 1) * width)
            total = h_ref[:, cols].astype(F32)
            for k in range(routes_each):
                at = b * picks + k * tok
                total += w_ref[0, k * tok : (k + 1) * tok, :1] * got[at : at + tok]
            total = jnp.where(section <= step, total, t_ref[:, cols].astype(F32))
            for home, f_ref in enumerate(rest[:-1]):
                total = jnp.where(section == home, f_ref[:, cols].astype(F32), total)
            o_ref[:, cols] = total.astype(BF16)

    whole = lambda i, s: (0, 0)
    chosen = lambda i, s: (batch_at(step, s, batches), 0, 0)
    return pl.pallas_call(
        kernel,
        out_shape=jax.ShapeDtypeStruct((tok, full), BF16),
        grid_spec=pltpu.PrefetchScalarGridSpec(
            num_scalar_prefetch=1,
            grid=(1,),
            in_specs=[
                pl.BlockSpec((rows, width), whole),
                pl.BlockSpec((1,) + spread.shape[1:], chosen),
                pl.BlockSpec((1, picks, 128), chosen),
            ]
            + [pl.BlockSpec((tok, full), whole)] * (2 + len(finished)),
            out_specs=pl.BlockSpec((tok, full), whole),
        ),
        compiler_params=params(),
        cost_estimate=cost(2 * spread.shape[1] * rows * width, 2 * rows * width),
    )(place, returned, spread, scales, hidden, tokens, *finished)


def per_device(tokens, norm_gain, gate_weight, up_weight, down_weight, routes, route_weights):
    sections = lax.axis_size("section")
    devices = lax.axis_size("expert")
    experts = devices // SHARDS
    _, batches, tok, routes_each = routes.shape
    full = tokens.shape[2]
    capacity = min(tok, tok * routes_each * 3 // (2 * experts))
    width = full // (2 * PARTS)
    section = lax.axis_index("section")
    core = lax.axis_index("expert") % 2
    place = jnp.stack([section, core]).astype(jnp.int32)
    own = tokens[0]

    slots = experts * capacity
    ids = jnp.moveaxis(routes[0], 2, 1).reshape(batches, routes_each * tok)
    order = jnp.arange(routes_each * tok)
    same = (ids[:, :, None] == ids[:, None, :]) & (order[None, :] < order[:, None])
    code = ids * capacity + jnp.sum(same.astype(jnp.int32), axis=2)
    blocks = jnp.arange(2 * PARTS, dtype=jnp.int32)
    keys = code.reshape(batches, routes_each, 1, tok) + (blocks * slots)[:, None]
    keys = keys.reshape(batches, routes_each, -1)
    unit = PARTS * capacity
    row = np.arange(devices * unit // 2)
    row_keys = (row // unit % 2 * PARTS + row % unit // capacity) * slots
    row_keys = row_keys + row // (2 * unit) * capacity + row % capacity
    sent = np.repeat(row_keys.reshape(experts, 1, 2 * unit), 2, axis=1).reshape(-1)
    row_keys = jnp.asarray(np.repeat(row_keys[:, None], keys.shape[2], axis=1), jnp.int32)
    wants = code[:, None, :] + (blocks * slots)[:, None]
    spread = (wants[:, :, :, None] == jnp.asarray(sent, jnp.int32)).reshape(batches, -1, sent.size).astype(BF16)
    scales = jnp.moveaxis(route_weights[0], 2, 1).reshape(batches, tok * routes_each, 1)
    scales = jnp.broadcast_to(scales, scales.shape[:2] + (128,))

    group = 8 * PARTS * capacity
    at = jnp.arange(group, dtype=jnp.int32)
    wanted = (at % (8 * capacity)) // capacity * (PARTS * capacity) + at // (8 * capacity) * capacity + at % capacity
    perm = (wanted[:, None] == at[None, :]).astype(BF16)
    back = (at[:, None] == wanted[None, :]).astype(BF16)

    swap = [(i, i ^ 1) for i in range(devices)]
    place, keys, row_keys, spread, scales, perm, back = lax.optimization_barrier(
        (place, keys, row_keys, spread, scales, perm, back)
    )
    gate, up, down = gate_weight, up_weight, down_weight
    hidden = own
    finished = []
    for step in range(batches + sections - 1):
        if step > 0:
            begins = max(0, step - batches)
            pairs = [(i, i + 1) for i in range(begins, min(step, sections - 1))]
            if step < batches:
                pairs.append((step, 0))
            else:
                pairs.append((sections - 1, step - batches))
            hidden = lax.ppermute(current, "section", pairs)
            if step >= batches:
                finished.append(hidden)
        packed = front(place, hidden, norm_gain, keys, row_keys, step, width=width, experts=experts)
        arrived = lax.all_to_all(packed, "expert", split_axis=0, concat_axis=0, tiled=True)
        others = lax.ppermute(arrived, "expert", swap)
        stage = step == 0
        sum_gate, sum_up, gate, up = first_half(place, arrived, perm, gate, up, stage)
        leaving, inner, down = second_half(
            place, others, perm, back, gate, up, down, sum_gate, sum_up, stage
        )
        received = lax.ppermute(leaving, "expert", swap)
        staying = own_down(place, inner, down, back)
        partial_value = (staying.astype(F32) + received.astype(F32)).astype(BF16)
        returned = lax.all_to_all(partial_value, "expert", split_axis=0, concat_axis=0, tiled=True)
        is_last = step == batches + sections - 2
        current = combine(
            place, returned, spread, scales, hidden, own, step, finished if is_last else ()
        )
    return current[None]


def solution(mesh):
    return jax.shard_map(
        per_device,
        mesh=mesh,
        in_specs=(
            P("section", "expert", None),
            P("section", None),
            P("section", None, "expert"),
            P("section", None, "expert"),
            P("section", "expert", None),
            P("section", None, "expert", None),
            P("section", None, "expert", None),
        ),
        out_specs=P("section", "expert", None),
        check_vma=False,
    )
```

```python
import jax
import jax.numpy as jnp
import numpy as np
from jax import lax
from jax.experimental import pallas as pl
from jax.experimental.pallas import tpu as pltpu
from jax.sharding import PartitionSpec as P

SHARDS = 4
PARTS = 4

F32 = jnp.float32
BF16 = jnp.bfloat16


SMEM_IN = pl.BlockSpec(memory_space=pltpu.SMEM)
VMEM_IN = pl.BlockSpec(memory_space=pltpu.VMEM)


def params():
    return pltpu.CompilerParams(vmem_limit_bytes=12 * 1024 * 1024)


def cost(flops, bytes_accessed):
    return pl.CostEstimate(flops=int(flops), bytes_accessed=int(bytes_accessed), transcendentals=0)


def mm(a, b):
    return jnp.dot(a, b, preferred_element_type=F32)


def batch_at(step, place, batches):
    return jnp.clip(step - place[0], 0, batches - 1)


def front(place, hidden, gain, keys, row_keys, step, *, width, experts):
    tok, full = hidden.shape
    batches, routes_each, lanes = keys.shape
    rows = row_keys.shape[0]
    blocks = full // width
    piece = rows // experts

    def kernel(place_ref, h_ref, g_ref, k_ref, r_ref, o_ref):
        x = h_ref[...].astype(F32)
        scale = lax.rsqrt(jnp.mean(x * x, axis=-1, keepdims=True) + 1e-06)
        normed = (x * scale * g_ref[...]).astype(BF16)
        stack = jnp.concatenate([normed[:, b * width : (b + 1) * width] for b in range(blocks)], axis=0)
        wanted = k_ref[batch_at(step, place_ref, batches)]
        hit = r_ref[...] == wanted[:1]
        for k in range(1, routes_each):
            hit |= r_ref[...] == wanted[k : k + 1]
        out = mm(jnp.where(hit, 1.0, 0.0).astype(BF16), stack).astype(BF16)
        for e in range(experts):
            for chip in range(2):
                at = (2 * e + chip) * piece
                o_ref[at : at + piece, :] = out[e * piece : (e + 1) * piece]

    return pl.pallas_call(
        kernel,
        out_shape=jax.ShapeDtypeStruct((2 * rows, width), BF16),
        in_specs=[SMEM_IN] + [VMEM_IN] * 4,
        out_specs=VMEM_IN,
        compiler_params=params(),
        cost_estimate=cost(2 * rows * lanes * width, 4 * rows * width),
    )(place, hidden, gain, keys, row_keys)


def held(array):
    return pltpu.with_memory_space_constraint(array, pltpu.VMEM)


def unpack(packed_ref, perm, xs, rows):
    group, width = perm.shape[0], packed_ref.shape[1]
    piece = group // PARTS
    for g in range(rows // piece):
        moved = mm(perm, packed_ref[g * group : (g + 1) * group, :]).astype(BF16)
        for b in range(PARTS):
            xs[g * piece : (g + 1) * piece, b * width : (b + 1) * width] = moved[b * piece : (b + 1) * piece]


def halves(core, depth):
    own = pl.ds(pl.multiple_of(core * depth, depth), depth)
    other = pl.ds(pl.multiple_of((1 - core) * depth, depth), depth)
    return own, other


def in_hbm(array):
    return pltpu.with_memory_space_constraint(array, pltpu.HBM)


HBM_IN = pl.BlockSpec(memory_space=pltpu.HBM)


def first_half(place, arrived, perm, gate, up, stage):
    all_rows, width = arrived.shape
    rows = all_rows // PARTS
    units = gate.shape[2]
    depth = PARTS * width

    def product(core, xs, g_ref, u_ref, og_ref, ou_ref):
        own, _ = halves(core, depth)
        og_ref[...] = mm(xs[...], g_ref[0, own, :])
        ou_ref[...] = mm(xs[...], u_ref[0, own, :])

    def kernel(place_ref, a_ref, p_ref, g_ref, u_ref, og_ref, ou_ref, xs):
        unpack(a_ref, p_ref[...], xs, rows)
        product(place_ref[1], xs, g_ref, u_ref, og_ref, ou_ref)

    def staging(place_ref, a_ref, p_ref, g_hbm, u_hbm, og_ref, ou_ref, g_ref, u_ref, xs, sems):
        core = place_ref[1]
        copies = []
        for part in halves(core, depth):
            for source, target in ((g_hbm, g_ref), (u_hbm, u_ref)):
                copy = pltpu.make_async_copy(source.at[0, part, :], target.at[0, part, :], sems.at[len(copies)])
                copy.start()
                copies.append(copy)
        unpack(a_ref, p_ref[...], xs, rows)
        copies[0].wait()
        copies[1].wait()
        product(core, xs, g_ref, u_ref, og_ref, ou_ref)
        copies[2].wait()
        copies[3].wait()

    sums = [jax.ShapeDtypeStruct((rows, units), F32)] * 2
    scratch = [pltpu.VMEM((rows, depth), BF16)]
    flops = 4 * all_rows * width * units
    if stage:
        return pl.pallas_call(
            staging,
            out_shape=sums + [pltpu.VMEM(gate.shape, BF16)] * 2,
            in_specs=[SMEM_IN] + [VMEM_IN] * 2 + [HBM_IN] * 2,
            out_specs=[VMEM_IN] * 4,
            scratch_shapes=scratch + [pltpu.SemaphoreType.DMA((4,))],
            compiler_params=params(),
            cost_estimate=cost(flops, 8 * gate.size),
        )(place, arrived, perm, in_hbm(gate), in_hbm(up))
    return pl.pallas_call(
        kernel,
        out_shape=sums,
        in_specs=[SMEM_IN] + [VMEM_IN] * 4,
        out_specs=[VMEM_IN] * 2,
        scratch_shapes=scratch,
        compiler_params=params(),
        cost_estimate=cost(flops, 2 * gate.size),
    )(place, arrived, perm, held(gate), held(up)) + (gate, up)


def second_half(place, arrived, perm, gate, up, sum_gate, sum_up, down, others_down, stage):
    all_rows, width = arrived.shape
    rows = all_rows // PARTS
    units = gate.shape[2]
    depth = PARTS * width

    def product(core, a_ref, p_ref, g_ref, u_ref, sg_ref, su_ref, i_ref, xs):
        unpack(a_ref, p_ref[...], xs, rows)
        _, other = halves(core, depth)
        pre = sg_ref[...] + mm(xs[...], g_ref[0, other, :])
        upper = su_ref[...] + mm(xs[...], u_ref[0, other, :])
        i_ref[...] = (pre * lax.logistic(pre) * upper).astype(BF16)

    def kernel(place_ref, *refs):
        product(place_ref[1], *refs)

    def staging(place_ref, a_ref, p_ref, g_ref, u_ref, sg_ref, su_ref, own_hbm, other_hbm, i_ref, d_ref, xs, sems):
        core = place_ref[1]
        own, _ = halves(core, depth)
        copies = [
            pltpu.make_async_copy(source.at[0, :, own], d_ref.at[n], sems.at[n])
            for n, source in enumerate((own_hbm, other_hbm))
        ]
        for copy in copies:
            copy.start()
        product(core, a_ref, p_ref, g_ref, u_ref, sg_ref, su_ref, i_ref, xs)
        for copy in copies:
            copy.wait()

    inner = jax.ShapeDtypeStruct((rows, units), BF16)
    scratch = [pltpu.VMEM((rows, depth), BF16)]
    estimate = cost(4 * all_rows * width * units, 2 * gate.size)
    operands = (place, arrived, perm, held(gate), held(up), sum_gate, sum_up)
    if stage:
        return pl.pallas_call(
            staging,
            out_shape=[inner, pltpu.VMEM((2, units, depth), BF16)],
            in_specs=[SMEM_IN] + [VMEM_IN] * 6 + [HBM_IN] * 2,
            out_specs=[VMEM_IN] * 2,
            scratch_shapes=scratch + [pltpu.SemaphoreType.DMA((2,))],
            compiler_params=params(),
            cost_estimate=estimate,
        )(*operands, in_hbm(down), in_hbm(others_down))
    return pl.pallas_call(
        kernel,
        out_shape=inner,
        in_specs=[SMEM_IN] + [VMEM_IN] * 6,
        out_specs=VMEM_IN,
        scratch_shapes=scratch,
        compiler_params=params(),
        cost_estimate=estimate,
    )(*operands), down


def own_units(inner, down):
    rows, units = inner.shape
    depth = down.shape[2]
    piece = depth // PARTS

    def kernel(i_ref, d_ref, o_ref):
        for b in range(PARTS):
            cols = slice(b * piece, (b + 1) * piece)
            o_ref[:, cols] = mm(i_ref[...], d_ref[0, :, cols])

    return pl.pallas_call(
        kernel,
        out_shape=jax.ShapeDtypeStruct((rows, depth), F32),
        in_specs=[VMEM_IN] * 2,
        out_specs=VMEM_IN,
        compiler_params=params(),
        cost_estimate=cost(2 * rows * units * depth, 2 * units * depth),
    )(inner, held(down))


def other_units(inner, down, total, back, width):
    rows = inner.shape[0]
    group = back.shape[0]
    piece = group // PARTS

    def kernel(i_ref, d_ref, t_ref, q_ref, o_ref, ys):
        for b in range(PARTS):
            cols = slice(b * width, (b + 1) * width)
            ys[b] = (t_ref[:, cols] + mm(i_ref[...], d_ref[1, :, cols])).astype(BF16)
        for g in range(rows // piece):
            stack = jnp.concatenate([ys[b, g * piece : (g + 1) * piece, :] for b in range(PARTS)], axis=0)
            o_ref[g * group : (g + 1) * group, :] = mm(q_ref[...], stack).astype(BF16)

    return pl.pallas_call(
        kernel,
        out_shape=jax.ShapeDtypeStruct((rows * PARTS, width), BF16),
        in_specs=[VMEM_IN] * 4,
        out_specs=VMEM_IN,
        scratch_shapes=[pltpu.VMEM((PARTS, rows, width), BF16)],
        compiler_params=params(),
        cost_estimate=cost(2 * inner.size * PARTS * width, inner.size),
    )(inner, held(down), total, back)


def combine(place, returned, spread, scales, hidden, tokens, step, finished=()):
    rows, width = returned.shape
    tok, full = hidden.shape
    batches = spread.shape[0]
    blocks = full // width
    picks = spread.shape[1] // blocks
    routes_each = picks // tok

    def kernel(place_ref, r_ref, s_ref, w_ref, h_ref, t_ref, *rest):
        o_ref = rest[-1]
        batch = batch_at(step, place_ref, batches)
        got = mm(s_ref[batch], r_ref[...])
        scale = w_ref[batch][:, :1]
        section = place_ref[0]
        for b in range(blocks):
            cols = slice(b * width, (b + 1) * width)
            total = h_ref[:, cols].astype(F32)
            for k in range(routes_each):
                at = b * picks + k * tok
                total += scale[k * tok : (k + 1) * tok] * got[at : at + tok]
            total = jnp.where(section <= step, total, t_ref[:, cols].astype(F32))
            for home, f_ref in enumerate(rest[:-1]):
                total = jnp.where(section == home, f_ref[:, cols].astype(F32), total)
            o_ref[:, cols] = total.astype(BF16)

    return pl.pallas_call(
        kernel,
        out_shape=jax.ShapeDtypeStruct((tok, full), BF16),
        in_specs=[SMEM_IN] + [VMEM_IN] * (5 + len(finished)),
        out_specs=VMEM_IN,
        compiler_params=params(),
        cost_estimate=cost(2 * spread.shape[1] * rows * width, 2 * rows * width),
    )(place, returned, spread, scales, hidden, tokens, *finished)


def per_device(tokens, norm_gain, gate_weight, up_weight, down_weight, routes, route_weights):
    sections = lax.axis_size("section")
    devices = lax.axis_size("expert")
    experts = devices // SHARDS
    _, batches, tok, routes_each = routes.shape
    full = tokens.shape[2]
    capacity = min(tok, tok * routes_each * 3 // (2 * experts))
    width = full // (2 * PARTS)
    section = lax.axis_index("section")
    core = lax.axis_index("expert") % 2
    place = jnp.stack([section, core]).astype(jnp.int32)
    own = tokens[0]

    slots = experts * capacity
    ids = jnp.moveaxis(routes[0], 2, 1).reshape(batches, routes_each * tok)
    order = jnp.arange(routes_each * tok)
    same = (ids[:, :, None] == ids[:, None, :]) & (order[None, :] < order[:, None])
    code = ids * capacity + jnp.sum(same.astype(jnp.int32), axis=2)
    blocks = jnp.arange(2 * PARTS, dtype=jnp.int32)
    keys = code.reshape(batches, routes_each, 1, tok) + (blocks * slots)[:, None]
    keys = keys.reshape(batches, routes_each, -1)
    unit = PARTS * capacity
    row = np.arange(devices * unit // 2)
    row_keys = (row // unit % 2 * PARTS + row % unit // capacity) * slots
    row_keys = row_keys + row // (2 * unit) * capacity + row % capacity
    sent = np.repeat(row_keys.reshape(experts, 1, 2 * unit), 2, axis=1).reshape(-1)
    row_keys = jnp.asarray(np.repeat(row_keys[:, None], keys.shape[2], axis=1), jnp.int32)
    wants = code[:, None, :] + (blocks * slots)[:, None]
    spread = (wants[:, :, :, None] == jnp.asarray(sent, jnp.int32)).reshape(batches, -1, sent.size).astype(BF16)
    scales = jnp.moveaxis(route_weights[0], 2, 1).reshape(batches, tok * routes_each, 1)
    scales = jnp.broadcast_to(scales, scales.shape[:2] + (128,))

    group = 8 * PARTS * capacity
    at = jnp.arange(group, dtype=jnp.int32)
    wanted = (at % (8 * capacity)) // capacity * (PARTS * capacity) + at // (8 * capacity) * capacity + at % capacity
    perm = (wanted[:, None] == at[None, :]).astype(BF16)
    back = (at[:, None] == wanted[None, :]).astype(BF16)

    swap = [(i, i ^ 1) for i in range(devices)]
    place, keys, row_keys, spread, scales, perm, back = lax.optimization_barrier(
        (place, keys, row_keys, spread, scales, perm, back)
    )
    gate, up, down = gate_weight, up_weight, down_weight
    others_down = lax.ppermute(down_weight, "expert", swap)
    hidden = own
    finished = []
    for step in range(batches + sections - 1):
        if step > 0:
            begins = max(0, step - batches)
            pairs = [(i, i + 1) for i in range(begins, min(step, sections - 1))]
            if step < batches:
                pairs.append((step, 0))
            else:
                pairs.append((sections - 1, step - batches))
            hidden = lax.ppermute(current, "section", pairs)
            if step >= batches:
                finished.append(hidden)
        packed = front(place, hidden, norm_gain, keys, row_keys, step, width=width, experts=experts)
        arrived = lax.all_to_all(packed, "expert", split_axis=0, concat_axis=0, tiled=True)
        others = lax.ppermute(arrived, "expert", swap)
        stage = step == 0
        sum_gate, sum_up, gate, up = first_half(place, arrived, perm, gate, up, stage)
        inner, down = second_half(
            place, others, perm, gate, up, sum_gate, sum_up, down, others_down, stage
        )
        others_inner = lax.ppermute(inner, "expert", swap)
        total = own_units(inner, down)
        partial_value = other_units(others_inner, down, total, back, width)
        returned = lax.all_to_all(partial_value, "expert", split_axis=0, concat_axis=0, tiled=True)
        is_last = step == batches + sections - 2
        current = combine(
            place, returned, spread, scales, hidden, own, step, finished if is_last else ()
        )
    return current[None]


def solution(mesh):
    return jax.shard_map(
        per_device,
        mesh=mesh,
        in_specs=(
            P("section", "expert", None),
            P("section", None),
            P("section", None, "expert"),
            P("section", None, "expert"),
            P("section", "expert", None),
            P("section", None, "expert", None),
            P("section", None, "expert", None),
        ),
        out_specs=P("section", "expert", None),
        check_vma=False,
    )
```

```python
import jax
import jax.numpy as jnp
import numpy as np
from jax import lax
from jax.experimental import pallas as pl
from jax.experimental.pallas import tpu as pltpu
from jax.sharding import PartitionSpec as P

SHARDS = 4
SECTIONS = 4
PARTS = 4

F32 = jnp.float32
BF16 = jnp.bfloat16


SMEM_IN = pl.BlockSpec(memory_space=pltpu.SMEM)
VMEM_IN = pl.BlockSpec(memory_space=pltpu.VMEM)


HBM_IN = pl.BlockSpec(memory_space=pltpu.HBM)


def in_hbm(array):
    return pltpu.with_memory_space_constraint(array, pltpu.HBM)


def params():
    return pltpu.CompilerParams(vmem_limit_bytes=12 * 1024 * 1024)


def cost(flops, bytes_accessed):
    return pl.CostEstimate(flops=int(flops), bytes_accessed=int(bytes_accessed), transcendentals=0)


def mm(a, b):
    return jnp.dot(a, b, preferred_element_type=F32)


def batch_at(step, place, batches):
    return jnp.clip(step - place[0], 0, batches - 1)


def plan(ids_ref, w_ref, sent_ref, k_ref, s_ref, c_ref, slots, capacity):
    batches, routes_each, tok = ids_ref.shape
    lanes = k_ref.shape[2]
    picks = routes_each * tok
    sub = lax.broadcasted_iota(jnp.int32, (tok, tok), 0)
    lane = lax.broadcasted_iota(jnp.int32, (tok, tok), 1)
    wide_sub = lax.broadcasted_iota(jnp.int32, (tok, lanes), 0)
    wide_lane = lax.broadcasted_iota(jnp.int32, (tok, lanes), 1)

    def column(values):
        values = jnp.broadcast_to(values, (tok, tok))
        return jnp.sum(jnp.where(sub == lane, values, jnp.zeros_like(values)), axis=1, keepdims=True)

    for m in range(batches):
        rows = [ids_ref[m, k : k + 1, :] for k in range(routes_each)]
        for k in range(routes_each):
            own = column(rows[k])
            code = own * capacity
            for before in range(k + 1):
                same = own == rows[before]
                if before == k:
                    same &= lane < sub
                code += jnp.sum(jnp.where(same, 1, 0), axis=1, keepdims=True)
            lane_code = jnp.sum(jnp.where(wide_sub == wide_lane % tok, code, 0), axis=0, keepdims=True)
            k_ref[m, k : k + 1, :] = lane_code + wide_lane[:1] // tok * slots
            for b in range(2 * PARTS):
                at = b * picks + k * tok
                hit = code + b * slots == sent_ref[...]
                s_ref[m, at : at + tok, :] = jnp.where(hit, 1.0, 0.0).astype(BF16)
            scale = column(w_ref[m, k : k + 1, :])
            c_ref[m, k * tok : (k + 1) * tok, :] = jnp.broadcast_to(scale, (tok, 128))


def pack(batch, h_ref, g_ref, k_ref, r_ref, o_ref, experts):
    rows = r_ref.shape[0]
    width = o_ref.shape[1]
    piece = rows // experts
    x = h_ref[...].astype(F32)
    scale = lax.rsqrt(jnp.mean(x * x, axis=-1, keepdims=True) + 1e-06)
    normed = (x * scale * g_ref[...]).astype(BF16)
    stack = jnp.concatenate([normed[:, b * width : (b + 1) * width] for b in range(2 * PARTS)], axis=0)
    wanted = k_ref[batch]
    hit = r_ref[...] == wanted[:1]
    for k in range(1, wanted.shape[0]):
        hit |= r_ref[...] == wanted[k : k + 1]
    out = mm(jnp.where(hit, 1.0, 0.0).astype(BF16), stack).astype(BF16)
    for e in range(experts):
        for chip in range(2):
            at = (2 * e + chip) * piece
            o_ref[at : at + piece, :] = out[e * piece : (e + 1) * piece]


def begin(place, tokens, gain, row_keys, ids, weights, sent, slots, capacity, experts):
    batches, routes_each, tok = ids.shape
    rows, lanes = row_keys.shape
    picks = routes_each * tok
    full = tokens.shape[1]

    def kernel(place_ref, *refs):
        sources, rest = refs[:6], refs[6:]
        h_ref, g_ref, r_ref, k_ref, s_ref, c_ref, o_ref, ids_ref, w_ref, sent_ref, sems = rest
        targets = (h_ref, g_ref, r_ref, ids_ref, w_ref, sent_ref)
        copies = [pltpu.make_async_copy(sources[i], targets[i], sems.at[i]) for i in range(6)]
        for copy in copies:
            copy.start()
        for copy in copies[3:]:
            copy.wait()
        plan(ids_ref, w_ref, sent_ref, k_ref, s_ref, c_ref, slots, capacity)
        for copy in copies[:3]:
            copy.wait()
        pack(batch_at(0, place_ref, batches), h_ref, g_ref, k_ref, r_ref, o_ref, experts)

    sources = (tokens, gain, row_keys, ids, weights, sent)
    return pl.pallas_call(
        kernel,
        out_shape=[
            pltpu.VMEM(tokens.shape, BF16),
            pltpu.VMEM(gain.shape, F32),
            pltpu.VMEM(row_keys.shape, jnp.int32),
            jax.ShapeDtypeStruct((batches, routes_each, lanes), jnp.int32),
            jax.ShapeDtypeStruct((batches, 2 * PARTS * picks, sent.shape[1]), BF16),
            jax.ShapeDtypeStruct((batches, picks, 128), F32),
            jax.ShapeDtypeStruct((2 * rows, full // (2 * PARTS)), BF16),
        ],
        in_specs=[SMEM_IN] + [HBM_IN] * 6,
        out_specs=[VMEM_IN] * 7,
        scratch_shapes=[
            pltpu.VMEM(ids.shape, jnp.int32),
            pltpu.VMEM(weights.shape, F32),
            pltpu.VMEM(sent.shape, jnp.int32),
            pltpu.SemaphoreType.DMA((6,)),
        ],
        compiler_params=params(),
    )(place, *[in_hbm(array) for array in sources])


def front(place, hidden, gain, keys, row_keys, step, *, width, experts):
    batches = keys.shape[0]
    rows, lanes = row_keys.shape

    def kernel(place_ref, *refs):
        pack(batch_at(step, place_ref, batches), *refs, experts)

    return pl.pallas_call(
        kernel,
        out_shape=jax.ShapeDtypeStruct((2 * rows, width), BF16),
        in_specs=[SMEM_IN] + [VMEM_IN] * 4,
        out_specs=VMEM_IN,
        compiler_params=params(),
        cost_estimate=cost(2 * rows * lanes * width, 4 * rows * width),
    )(place, hidden, gain, keys, row_keys)


def held(array):
    return pltpu.with_memory_space_constraint(array, pltpu.VMEM)


def unpack(packed_ref, perm, xs, rows):
    group, width = perm.shape[0], packed_ref.shape[1]
    piece = group // PARTS
    for g in range(rows // piece):
        moved = mm(perm, packed_ref[g * group : (g + 1) * group, :]).astype(BF16)
        for b in range(PARTS):
            xs[g * piece : (g + 1) * piece, b * width : (b + 1) * width] = moved[b * piece : (b + 1) * piece]


def halves(core, depth):
    own = pl.ds(pl.multiple_of(core * depth, depth), depth)
    other = pl.ds(pl.multiple_of((1 - core) * depth, depth), depth)
    return own, other


def first_half(place, arrived, perm, gate, up, stage):
    all_rows, width = arrived.shape
    rows = all_rows // PARTS
    units = gate.shape[2]
    depth = PARTS * width

    def product(core, xs, g_ref, u_ref, og_ref, ou_ref):
        own, _ = halves(core, depth)
        og_ref[...] = mm(xs[...], g_ref[0, own, :])
        ou_ref[...] = mm(xs[...], u_ref[0, own, :])

    def kernel(place_ref, a_ref, p_ref, g_ref, u_ref, og_ref, ou_ref, xs):
        unpack(a_ref, p_ref[...], xs, rows)
        product(place_ref[1], xs, g_ref, u_ref, og_ref, ou_ref)

    def staging(place_ref, a_ref, p_ref, g_hbm, u_hbm, og_ref, ou_ref, g_ref, u_ref, xs, sems):
        core = place_ref[1]
        copies = []
        for part in halves(core, depth):
            for source, target in ((g_hbm, g_ref), (u_hbm, u_ref)):
                copy = pltpu.make_async_copy(source.at[0, part, :], target.at[0, part, :], sems.at[len(copies)])
                copy.start()
                copies.append(copy)
        unpack(a_ref, p_ref[...], xs, rows)
        copies[0].wait()
        copies[1].wait()
        product(core, xs, g_ref, u_ref, og_ref, ou_ref)
        copies[2].wait()
        copies[3].wait()

    sums = [jax.ShapeDtypeStruct((rows, units), F32)] * 2
    scratch = [pltpu.VMEM((rows, depth), BF16)]
    flops = 4 * all_rows * width * units
    if stage:
        return pl.pallas_call(
            staging,
            out_shape=sums + [pltpu.VMEM(gate.shape, BF16)] * 2,
            in_specs=[SMEM_IN] + [VMEM_IN] * 2 + [HBM_IN] * 2,
            out_specs=[VMEM_IN] * 4,
            scratch_shapes=scratch + [pltpu.SemaphoreType.DMA((4,))],
            compiler_params=params(),
            cost_estimate=cost(flops, 8 * gate.size),
        )(place, arrived, perm, in_hbm(gate), in_hbm(up))
    return pl.pallas_call(
        kernel,
        out_shape=sums,
        in_specs=[SMEM_IN] + [VMEM_IN] * 4,
        out_specs=[VMEM_IN] * 2,
        scratch_shapes=scratch,
        compiler_params=params(),
        cost_estimate=cost(flops, 2 * gate.size),
    )(place, arrived, perm, held(gate), held(up)) + (gate, up)


def second_half(place, arrived, perm, gate, up, sum_gate, sum_up, down, others_down, stage):
    all_rows, width = arrived.shape
    rows = all_rows // PARTS
    units = gate.shape[2]
    depth = PARTS * width

    def product(core, a_ref, p_ref, g_ref, u_ref, sg_ref, su_ref, i_ref, xs):
        unpack(a_ref, p_ref[...], xs, rows)
        _, other = halves(core, depth)
        pre = sg_ref[...] + mm(xs[...], g_ref[0, other, :])
        upper = su_ref[...] + mm(xs[...], u_ref[0, other, :])
        i_ref[...] = (pre * lax.logistic(pre) * upper).astype(BF16)

    def kernel(place_ref, *refs):
        product(place_ref[1], *refs)

    def staging(place_ref, a_ref, p_ref, g_ref, u_ref, sg_ref, su_ref, own_hbm, other_hbm, i_ref, d_ref, xs, sems):
        core = place_ref[1]
        own, _ = halves(core, depth)
        copies = [
            pltpu.make_async_copy(source.at[0, :, own], d_ref.at[n], sems.at[n])
            for n, source in enumerate((own_hbm, other_hbm))
        ]
        for copy in copies:
            copy.start()
        product(core, a_ref, p_ref, g_ref, u_ref, sg_ref, su_ref, i_ref, xs)
        for copy in copies:
            copy.wait()

    inner = jax.ShapeDtypeStruct((rows, units), BF16)
    scratch = [pltpu.VMEM((rows, depth), BF16)]
    estimate = cost(4 * all_rows * width * units, 2 * gate.size)
    operands = (place, arrived, perm, held(gate), held(up), sum_gate, sum_up)
    if stage:
        return pl.pallas_call(
            staging,
            out_shape=[inner, pltpu.VMEM((2, units, depth), BF16)],
            in_specs=[SMEM_IN] + [VMEM_IN] * 6 + [HBM_IN] * 2,
            out_specs=[VMEM_IN] * 2,
            scratch_shapes=scratch + [pltpu.SemaphoreType.DMA((2,))],
            compiler_params=params(),
            cost_estimate=estimate,
        )(*operands, in_hbm(down), in_hbm(others_down))
    return pl.pallas_call(
        kernel,
        out_shape=inner,
        in_specs=[SMEM_IN] + [VMEM_IN] * 6,
        out_specs=VMEM_IN,
        scratch_shapes=scratch,
        compiler_params=params(),
        cost_estimate=estimate,
    )(*operands), down


def own_units(inner, down):
    rows, units = inner.shape
    depth = down.shape[2]
    piece = depth // PARTS

    def kernel(i_ref, d_ref, o_ref):
        for b in range(PARTS):
            cols = slice(b * piece, (b + 1) * piece)
            o_ref[:, cols] = mm(i_ref[...], d_ref[0, :, cols])

    return pl.pallas_call(
        kernel,
        out_shape=jax.ShapeDtypeStruct((rows, depth), F32),
        in_specs=[VMEM_IN] * 2,
        out_specs=VMEM_IN,
        compiler_params=params(),
        cost_estimate=cost(2 * rows * units * depth, 2 * units * depth),
    )(inner, held(down))


def other_units(inner, down, total, back, width):
    rows = inner.shape[0]
    group = back.shape[0]
    piece = group // PARTS

    def kernel(i_ref, d_ref, t_ref, q_ref, o_ref, ys):
        for b in range(PARTS):
            cols = slice(b * width, (b + 1) * width)
            ys[b] = (t_ref[:, cols] + mm(i_ref[...], d_ref[1, :, cols])).astype(BF16)
        for g in range(rows // piece):
            stack = jnp.concatenate([ys[b, g * piece : (g + 1) * piece, :] for b in range(PARTS)], axis=0)
            o_ref[g * group : (g + 1) * group, :] = mm(q_ref[...], stack).astype(BF16)

    return pl.pallas_call(
        kernel,
        out_shape=jax.ShapeDtypeStruct((rows * PARTS, width), BF16),
        in_specs=[VMEM_IN] * 4,
        out_specs=VMEM_IN,
        scratch_shapes=[pltpu.VMEM((PARTS, rows, width), BF16)],
        compiler_params=params(),
        cost_estimate=cost(2 * inner.size * PARTS * width, inner.size),
    )(inner, held(down), total, back)


def combine(place, returned, spread, scales, hidden, tokens, step, finished=()):
    rows, width = returned.shape
    tok, full = hidden.shape
    batches = spread.shape[0]
    blocks = full // width
    picks = spread.shape[1] // blocks
    routes_each = picks // tok

    def kernel(place_ref, r_ref, s_ref, w_ref, h_ref, t_ref, *rest):
        o_ref = rest[-1]
        batch = batch_at(step, place_ref, batches)
        got = mm(s_ref[batch], r_ref[...])
        scale = w_ref[batch][:, :1]
        section = place_ref[0]
        for b in range(blocks):
            cols = slice(b * width, (b + 1) * width)
            total = h_ref[:, cols].astype(F32)
            for k in range(routes_each):
                at = b * picks + k * tok
                total += scale[k * tok : (k + 1) * tok] * got[at : at + tok]
            if step < SECTIONS - 1:
                waiting = h_ref if step == 1 else t_ref
                total = jnp.where(section > step, waiting[:, cols].astype(F32), total)
            if step >= batches:
                total = jnp.where(section <= step - batches, h_ref[:, cols].astype(F32), total)
            if finished:
                total = jnp.where(section < SECTIONS - 1, rest[1][:, cols].astype(F32), total)
                total = jnp.where(section == 0, rest[0][:, cols].astype(F32), total)
            o_ref[:, cols] = total.astype(BF16)

    return pl.pallas_call(
        kernel,
        out_shape=jax.ShapeDtypeStruct((tok, full), BF16),
        in_specs=[SMEM_IN] + [VMEM_IN] * (5 + len(finished)),
        out_specs=VMEM_IN,
        compiler_params=params(),
        cost_estimate=cost(2 * spread.shape[1] * rows * width, 2 * rows * width),
    )(place, returned, spread, scales, hidden, tokens, *finished)


def per_device(tokens, norm_gain, gate_weight, up_weight, down_weight, routes, route_weights):
    sections = lax.axis_size("section")
    devices = lax.axis_size("expert")
    experts = devices // SHARDS
    _, batches, tok, routes_each = routes.shape
    full = tokens.shape[2]
    capacity = min(tok, tok * routes_each * 3 // (2 * experts))
    width = full // (2 * PARTS)
    section = lax.axis_index("section")
    core = lax.axis_index("expert") % 2
    place = jnp.stack([section, core]).astype(jnp.int32)

    slots = experts * capacity
    unit = PARTS * capacity
    row = np.arange(devices * unit // 2)
    row_keys = (row // unit % 2 * PARTS + row % unit // capacity) * slots
    row_keys = row_keys + row // (2 * unit) * capacity + row % capacity
    sent = np.repeat(row_keys.reshape(experts, 1, 2 * unit), 2, axis=1).reshape(1, -1)
    row_keys = np.repeat(row_keys[:, None], 2 * PARTS * tok, axis=1)
    row_keys, sent = jnp.asarray(row_keys, jnp.int32), jnp.asarray(sent, jnp.int32)
    by_route = lambda array: jnp.moveaxis(array[0], 2, 1)
    own, gain, row_keys, keys, spread, scales, packed = begin(
        place, tokens[0], norm_gain, row_keys, by_route(routes), by_route(route_weights), sent, slots, capacity, experts
    )

    group = 8 * PARTS * capacity
    at = jnp.arange(group, dtype=jnp.int32)
    wanted = (at % (8 * capacity)) // capacity * (PARTS * capacity) + at // (8 * capacity) * capacity + at % capacity
    perm = (wanted[:, None] == at[None, :]).astype(BF16)
    back = (at[:, None] == wanted[None, :]).astype(BF16)

    swap = [(i, i ^ 1) for i in range(devices)]
    perm, back = lax.optimization_barrier((perm, back))
    gate, up, down = gate_weight, up_weight, down_weight
    others_down = lax.ppermute(down_weight, "expert", swap)
    hidden = own
    finished = []
    steps = batches + sections - 1
    for step in range(steps):
        if step > 0:
            if step in (1, steps - 1):
                pairs = [(i, i ^ 1) for i in range(sections)]
            else:
                pairs = [(i, (i + 1) % sections) for i in range(sections)]
            hidden = lax.ppermute(current, "section", pairs)
            if step in (batches, steps - 1):
                finished.append(hidden)
            packed = front(place, hidden, gain, keys, row_keys, step, width=width, experts=experts)
        arrived = lax.all_to_all(packed, "expert", split_axis=0, concat_axis=0, tiled=True)
        others = lax.ppermute(arrived, "expert", swap)
        stage = step == 0
        sum_gate, sum_up, gate, up = first_half(place, arrived, perm, gate, up, stage)
        inner, down = second_half(
            place, others, perm, gate, up, sum_gate, sum_up, down, others_down, stage
        )
        others_inner = lax.ppermute(inner, "expert", swap)
        total = own_units(inner, down)
        partial_value = other_units(others_inner, down, total, back, width)
        returned = lax.all_to_all(partial_value, "expert", split_axis=0, concat_axis=0, tiled=True)
        is_last = step == steps - 1
        current = combine(
            place, returned, spread, scales, hidden, own, step, finished if is_last else ()
        )
    return current[None]


def solution(mesh):
    return jax.shard_map(
        per_device,
        mesh=mesh,
        in_specs=(
            P("section", "expert", None),
            P("section", None),
            P("section", None, "expert"),
            P("section", None, "expert"),
            P("section", "expert", None),
            P("section", None, "expert", None),
            P("section", None, "expert", None),
        ),
        out_specs=P("section", "expert", None),
        check_vma=False,
    )
```

```python
import jax
import jax.numpy as jnp
import numpy as np
from jax import lax
from jax.experimental import pallas as pl
from jax.experimental.pallas import tpu as pltpu
from jax.sharding import PartitionSpec as P

SHARDS = 4
COMPUTED, TOKENS, SENT, FIRST, NEXT = range(5)
SECTIONS = 4
PARTS = 4

F32 = jnp.float32
BF16 = jnp.bfloat16


SMEM_IN = pl.BlockSpec(memory_space=pltpu.SMEM)
VMEM_IN = pl.BlockSpec(memory_space=pltpu.VMEM)


HBM_IN = pl.BlockSpec(memory_space=pltpu.HBM)


def in_hbm(array):
    return pltpu.with_memory_space_constraint(array, pltpu.HBM)


def params():
    return pltpu.CompilerParams(vmem_limit_bytes=12 * 1024 * 1024)


def cost(flops, bytes_accessed):
    return pl.CostEstimate(flops=int(flops), bytes_accessed=int(bytes_accessed), transcendentals=0)


def mm(a, b):
    return jnp.dot(a, b, preferred_element_type=F32)


def plan(section, steps, ids_ref, w_ref, sent_ref, k_ref, s_ref, c_ref, m_ref, slots, capacity):
    batches, routes_each, tok = ids_ref.shape
    lanes = k_ref.shape[2]
    picks = routes_each * tok
    sub = lax.broadcasted_iota(jnp.int32, (tok, tok), 0)
    lane = lax.broadcasted_iota(jnp.int32, (tok, tok), 1)
    wide_sub = lax.broadcasted_iota(jnp.int32, (tok, lanes), 0)
    wide_lane = lax.broadcasted_iota(jnp.int32, (tok, lanes), 1)

    def column(values):
        values = jnp.broadcast_to(values, (tok, tok))
        return jnp.sum(jnp.where(sub == lane, values, jnp.zeros_like(values)), axis=1, keepdims=True)

    for step in range(steps):
        m = jnp.clip(step - section, 0, batches - 1)
        ids, weights = ids_ref[m], w_ref[m]
        rows = [ids[k : k + 1] for k in range(routes_each)]
        for k in range(routes_each):
            own = column(rows[k])
            code = own * capacity
            for before in range(k + 1):
                same = own == rows[before]
                if before == k:
                    same &= lane < sub
                code += jnp.sum(jnp.where(same, 1, 0), axis=1, keepdims=True)
            lane_code = jnp.sum(jnp.where(wide_sub == wide_lane % tok, code, 0), axis=0, keepdims=True)
            k_ref[step, k : k + 1, :] = lane_code + wide_lane[:1] // tok * slots
            for b in range(2 * PARTS):
                at = b * picks + k * tok
                hit = code + b * slots == sent_ref[...]
                s_ref[step, at : at + tok, :] = jnp.where(hit, 1.0, 0.0).astype(BF16)
            scale = column(weights[k : k + 1])
            c_ref[step, k * tok : (k + 1) * tok, :] = jnp.broadcast_to(scale, (tok, 128))
        mode = jnp.where(section > step, SENT if step == 1 else TOKENS, COMPUTED)
        mode = jnp.where(section <= step - batches, SENT, mode)
        if step == steps - 1:
            mode = jnp.where(section < SECTIONS - 1, jnp.where(section == 0, FIRST, NEXT), COMPUTED)
        m_ref[step] = jnp.full(m_ref.shape[1:], mode, jnp.int32)


def pack(step, h_ref, g_ref, k_ref, r_ref, o_ref, experts):
    rows = r_ref.shape[0]
    width = o_ref.shape[1]
    piece = rows // experts
    x = h_ref[...].astype(F32)
    scale = lax.rsqrt(jnp.mean(x * x, axis=-1, keepdims=True) + 1e-06)
    normed = (x * scale * g_ref[...]).astype(BF16)
    stack = jnp.concatenate([normed[:, b * width : (b + 1) * width] for b in range(2 * PARTS)], axis=0)
    wanted = k_ref[step]
    hit = r_ref[...] == wanted[:1]
    for k in range(1, wanted.shape[0]):
        hit |= r_ref[...] == wanted[k : k + 1]
    out = mm(jnp.where(hit, 1.0, 0.0).astype(BF16), stack).astype(BF16)
    for e in range(experts):
        for chip in range(2):
            at = (2 * e + chip) * piece
            o_ref[at : at + piece, :] = out[e * piece : (e + 1) * piece]


def begin(place, tokens, gain, row_keys, ids, weights, sent, slots, capacity, experts, steps):
    batches, routes_each, tok = ids.shape
    rows, lanes = row_keys.shape
    picks = routes_each * tok
    full = tokens.shape[1]

    def kernel(place_ref, *refs):
        sources, rest = refs[:6], refs[6:]
        h_ref, g_ref, r_ref, k_ref, s_ref, c_ref, m_ref, o_ref, ids_ref, w_ref, sent_ref, sems = rest
        targets = (h_ref, g_ref, r_ref, ids_ref, w_ref, sent_ref)
        copies = [pltpu.make_async_copy(sources[i], targets[i], sems.at[i]) for i in range(6)]
        for copy in copies:
            copy.start()
        for copy in copies[3:]:
            copy.wait()
        plan(place_ref[0], steps, ids_ref, w_ref, sent_ref, k_ref, s_ref, c_ref, m_ref, slots, capacity)
        for copy in copies[:3]:
            copy.wait()
        pack(0, h_ref, g_ref, k_ref, r_ref, o_ref, experts)

    sources = (tokens, gain, row_keys, ids, weights, sent)
    return pl.pallas_call(
        kernel,
        out_shape=[
            pltpu.VMEM(tokens.shape, BF16),
            pltpu.VMEM(gain.shape, F32),
            pltpu.VMEM(row_keys.shape, jnp.int32),
            pltpu.VMEM((steps, routes_each, lanes), jnp.int32),
            pltpu.VMEM((steps, 2 * PARTS * picks, sent.shape[1]), BF16),
            pltpu.VMEM((steps, picks, 128), F32),
            pltpu.VMEM((steps, 8, 128), jnp.int32),
            jax.ShapeDtypeStruct((2 * rows, full // (2 * PARTS)), BF16),
        ],
        in_specs=[SMEM_IN] + [HBM_IN] * 6,
        out_specs=[VMEM_IN] * 8,
        scratch_shapes=[
            pltpu.VMEM(ids.shape, jnp.int32),
            pltpu.VMEM(weights.shape, F32),
            pltpu.VMEM(sent.shape, jnp.int32),
            pltpu.SemaphoreType.DMA((6,)),
        ],
        compiler_params=params(),
    )(place, *[in_hbm(array) for array in sources])


def front(hidden, gain, keys, row_keys, step, *, width, experts):
    rows, lanes = row_keys.shape

    def kernel(*refs):
        pack(step, *refs, experts)

    return pl.pallas_call(
        kernel,
        out_shape=jax.ShapeDtypeStruct((2 * rows, width), BF16),
        in_specs=[VMEM_IN] * 4,
        out_specs=VMEM_IN,
        compiler_params=params(),
        cost_estimate=cost(2 * rows * lanes * width, 4 * rows * width),
    )(hidden, held(gain), held(keys), held(row_keys))


def held(array):
    return pltpu.with_memory_space_constraint(array, pltpu.VMEM)


def unpack(packed_ref, perm, xs, rows):
    group, width = perm.shape[0], packed_ref.shape[1]
    piece = group // PARTS
    for g in range(rows // piece):
        moved = mm(perm, packed_ref[g * group : (g + 1) * group, :]).astype(BF16)
        for b in range(PARTS):
            xs[g * piece : (g + 1) * piece, b * width : (b + 1) * width] = moved[b * piece : (b + 1) * piece]


def halves(core, depth):
    own = pl.ds(pl.multiple_of(core * depth, depth), depth)
    other = pl.ds(pl.multiple_of((1 - core) * depth, depth), depth)
    return own, other


def times(xs, weight_ref):
    return mm(xs[...], weight_ref[...])


def first_half(place, arrived, perm, gate, up, stage):
    all_rows, width = arrived.shape
    rows = all_rows // PARTS
    depth = PARTS * width
    units = gate.shape[-1]

    def kernel(a_ref, p_ref, g_ref, u_ref, og_ref, ou_ref, xs):
        unpack(a_ref, p_ref[...], xs, rows)
        og_ref[...] = times(xs, g_ref)
        ou_ref[...] = times(xs, u_ref)

    def staging(place_ref, a_ref, p_ref, g_hbm, u_hbm, og_ref, ou_ref, g_ref, u_ref, g_other, u_other, xs, sems):
        copies = []
        for part, targets in zip(halves(place_ref[1], depth), ((g_ref, u_ref), (g_other, u_other))):
            for source, target in zip((g_hbm, u_hbm), targets):
                copy = pltpu.make_async_copy(source.at[0, part, :], target, sems.at[len(copies)])
                copy.start()
                copies.append(copy)
        unpack(a_ref, p_ref[...], xs, rows)
        copies[0].wait()
        og_ref[...] = times(xs, g_ref)
        copies[1].wait()
        ou_ref[...] = times(xs, u_ref)
        copies[2].wait()
        copies[3].wait()

    sums = [jax.ShapeDtypeStruct((rows, units), F32)] * 2
    scratch = [pltpu.VMEM((rows, depth), BF16)]
    estimate = cost(4 * all_rows * width * units, 4 * depth * units)
    if stage:
        return pl.pallas_call(
            staging,
            out_shape=sums + [pltpu.VMEM((depth, units), BF16)] * 4,
            in_specs=[SMEM_IN] + [VMEM_IN] * 2 + [HBM_IN] * 2,
            out_specs=[VMEM_IN] * 6,
            scratch_shapes=scratch + [pltpu.SemaphoreType.DMA((4,))],
            compiler_params=params(),
            cost_estimate=estimate,
        )(place, arrived, perm, in_hbm(gate), in_hbm(up))
    return pl.pallas_call(
        kernel,
        out_shape=sums,
        in_specs=[VMEM_IN] * 4,
        out_specs=[VMEM_IN] * 2,
        scratch_shapes=scratch,
        compiler_params=params(),
        cost_estimate=estimate,
    )(arrived, perm, held(gate), held(up))


def second_half(place, arrived, perm, gate, up, sum_gate, sum_up, down, others_down, stage):
    all_rows, width = arrived.shape
    rows = all_rows // PARTS
    depth, units = gate.shape

    def kernel(a_ref, p_ref, g_ref, u_ref, sg_ref, su_ref, i_ref, xs):
        unpack(a_ref, p_ref[...], xs, rows)
        pre = sg_ref[...] + times(xs, g_ref)
        upper = su_ref[...] + times(xs, u_ref)
        i_ref[...] = (pre * lax.logistic(pre) * upper).astype(BF16)

    def staging(place_ref, a_ref, p_ref, g_ref, u_ref, sg_ref, su_ref, own_hbm, other_hbm, i_ref, d_ref, xs, sems):
        own, _ = halves(place_ref[1], depth)
        copies = [
            pltpu.make_async_copy(source.at[0, :, own], d_ref.at[n], sems.at[n])
            for n, source in enumerate((own_hbm, other_hbm))
        ]
        for copy in copies:
            copy.start()
        kernel(a_ref, p_ref, g_ref, u_ref, sg_ref, su_ref, i_ref, xs)
        for copy in copies:
            copy.wait()

    inner = jax.ShapeDtypeStruct((rows, units), BF16)
    scratch = [pltpu.VMEM((rows, depth), BF16)]
    estimate = cost(4 * all_rows * width * units, 4 * depth * units)
    operands = (arrived, perm, held(gate), held(up), sum_gate, sum_up)
    if stage:
        return pl.pallas_call(
            staging,
            out_shape=[inner, pltpu.VMEM((2, units, depth), BF16)],
            in_specs=[SMEM_IN] + [VMEM_IN] * 6 + [HBM_IN] * 2,
            out_specs=[VMEM_IN] * 2,
            scratch_shapes=scratch + [pltpu.SemaphoreType.DMA((2,))],
            compiler_params=params(),
            cost_estimate=estimate,
        )(place, *operands, in_hbm(down), in_hbm(others_down))
    return pl.pallas_call(
        kernel,
        out_shape=inner,
        in_specs=[VMEM_IN] * 6,
        out_specs=VMEM_IN,
        scratch_shapes=scratch,
        compiler_params=params(),
        cost_estimate=estimate,
    )(*operands), down


def own_units(inner, down):
    rows, units = inner.shape
    depth = down.shape[2]
    piece = depth // PARTS

    def kernel(i_ref, d_ref, o_ref):
        for b in range(PARTS):
            cols = slice(b * piece, (b + 1) * piece)
            o_ref[:, cols] = mm(i_ref[...], d_ref[0, :, cols])

    return pl.pallas_call(
        kernel,
        out_shape=jax.ShapeDtypeStruct((rows, depth), F32),
        in_specs=[VMEM_IN] * 2,
        out_specs=VMEM_IN,
        compiler_params=params(),
        cost_estimate=cost(2 * rows * units * depth, 2 * units * depth),
    )(inner, held(down))


def other_units(inner, down, total, back, width):
    rows = inner.shape[0]
    group = back.shape[0]
    piece = group // PARTS

    def kernel(i_ref, d_ref, t_ref, q_ref, o_ref, ys):
        for b in range(PARTS):
            cols = slice(b * width, (b + 1) * width)
            ys[b] = (t_ref[:, cols] + mm(i_ref[...], d_ref[1, :, cols])).astype(BF16)
        for g in range(rows // piece):
            stack = jnp.concatenate([ys[b, g * piece : (g + 1) * piece, :] for b in range(PARTS)], axis=0)
            o_ref[g * group : (g + 1) * group, :] = mm(q_ref[...], stack).astype(BF16)

    return pl.pallas_call(
        kernel,
        out_shape=jax.ShapeDtypeStruct((rows * PARTS, width), BF16),
        in_specs=[VMEM_IN] * 4,
        out_specs=VMEM_IN,
        scratch_shapes=[pltpu.VMEM((PARTS, rows, width), BF16)],
        compiler_params=params(),
        cost_estimate=cost(2 * inner.size * PARTS * width, inner.size),
    )(inner, held(down), total, back)


def combine(returned, spread, scales, modes, hidden, tokens, step, finished=()):
    rows, width = returned.shape
    tok, full = hidden.shape
    blocks = full // width
    picks = spread.shape[1] // blocks
    routes_each = picks // tok

    def kernel(r_ref, s_ref, w_ref, m_ref, h_ref, t_ref, *rest):
        o_ref = rest[-1]
        got = mm(s_ref[step], r_ref[...])
        scale = w_ref[step][:, :1]
        mode = jnp.broadcast_to(m_ref[step, :1, :1], (tok, 1))
        others = {TOKENS: t_ref, SENT: h_ref, **dict(zip((FIRST, NEXT), rest[:-1]))}
        for b in range(blocks):
            cols = slice(b * width, (b + 1) * width)
            total = h_ref[:, cols].astype(F32)
            for k in range(routes_each):
                at = b * picks + k * tok
                total += scale[k * tok : (k + 1) * tok] * got[at : at + tok]
            for kind, ref in others.items():
                total = jnp.where(mode == kind, ref[:, cols].astype(F32), total)
            o_ref[:, cols] = total.astype(BF16)

    return pl.pallas_call(
        kernel,
        out_shape=jax.ShapeDtypeStruct((tok, full), BF16),
        in_specs=[VMEM_IN] * (6 + len(finished)),
        out_specs=VMEM_IN,
        compiler_params=params(),
        cost_estimate=cost(2 * spread.shape[1] * rows * width, 2 * rows * width),
    )(returned, held(spread), held(scales), held(modes), hidden, held(tokens), *finished)


def per_device(tokens, norm_gain, gate_weight, up_weight, down_weight, routes, route_weights):
    sections = lax.axis_size("section")
    devices = lax.axis_size("expert")
    experts = devices // SHARDS
    _, batches, tok, routes_each = routes.shape
    full = tokens.shape[2]
    capacity = min(tok, tok * routes_each * 3 // (2 * experts))
    width = full // (2 * PARTS)
    section = lax.axis_index("section")
    core = lax.axis_index("expert") % 2
    place = jnp.stack([section, core]).astype(jnp.int32)

    slots = experts * capacity
    unit = PARTS * capacity
    row = np.arange(devices * unit // 2)
    row_keys = (row // unit % 2 * PARTS + row % unit // capacity) * slots
    row_keys = row_keys + row // (2 * unit) * capacity + row % capacity
    sent = np.repeat(row_keys.reshape(experts, 1, 2 * unit), 2, axis=1).reshape(1, -1)
    row_keys = np.repeat(row_keys[:, None], 2 * PARTS * tok, axis=1)
    row_keys, sent = jnp.asarray(row_keys, jnp.int32), jnp.asarray(sent, jnp.int32)
    by_route = lambda array: jnp.moveaxis(array[0], 2, 1)
    steps = batches + sections - 1
    own, gain, row_keys, keys, spread, scales, modes, packed = begin(
        place, tokens[0], norm_gain, row_keys, by_route(routes), by_route(route_weights), sent, slots, capacity, experts, steps
    )

    group = 8 * PARTS * capacity
    at = jnp.arange(group, dtype=jnp.int32)
    wanted = (at % (8 * capacity)) // capacity * (PARTS * capacity) + at // (8 * capacity) * capacity + at % capacity
    perm = (wanted[:, None] == at[None, :]).astype(BF16)
    back = (at[:, None] == wanted[None, :]).astype(BF16)

    swap = [(i, i ^ 1) for i in range(devices)]
    perm, back = lax.optimization_barrier((perm, back))
    gate, up, down = gate_weight, up_weight, down_weight
    others_down = lax.ppermute(down_weight, "expert", swap)
    hidden = own
    finished = []
    for step in range(steps):
        if step > 0:
            if step in (1, steps - 1):
                pairs = [(i, i ^ 1) for i in range(sections)]
            else:
                pairs = [(i, (i + 1) % sections) for i in range(sections)]
            hidden = lax.ppermute(current, "section", pairs)
            if step in (batches, steps - 1):
                finished.append(hidden)
            packed = front(hidden, gain, keys, row_keys, step, width=width, experts=experts)
        arrived = lax.all_to_all(packed, "expert", split_axis=0, concat_axis=0, tiled=True)
        others = lax.ppermute(arrived, "expert", swap)
        stage = step == 0
        sum_gate, sum_up, *staged = first_half(place, arrived, perm, gate, up, stage)
        if stage:
            gate, up, other_gate, other_up = staged
        inner, down = second_half(
            place, others, perm, other_gate, other_up, sum_gate, sum_up, down, others_down, stage
        )
        others_inner = lax.ppermute(inner, "expert", swap)
        total = own_units(inner, down)
        partial_value = other_units(others_inner, down, total, back, width)
        returned = lax.all_to_all(partial_value, "expert", split_axis=0, concat_axis=0, tiled=True)
        is_last = step == steps - 1
        current = combine(
            returned, spread, scales, modes, hidden, own, step, finished if is_last else ()
        )
    return current[None]


def solution(mesh):
    return jax.shard_map(
        per_device,
        mesh=mesh,
        in_specs=(
            P("section", "expert", None),
            P("section", None),
            P("section", None, "expert"),
            P("section", None, "expert"),
            P("section", "expert", None),
            P("section", None, "expert", None),
            P("section", None, "expert", None),
        ),
        out_specs=P("section", "expert", None),
        check_vma=False,
    )
```

```python
import jax
import jax.numpy as jnp
import numpy as np
from jax import lax
from jax.experimental import pallas as pl
from jax.experimental.pallas import tpu as pltpu
from jax.sharding import PartitionSpec as P

SHARDS = 4
COMPUTED, TOKENS, SENT = range(3)
SECTIONS = 4
PARTS = 4

F32 = jnp.float32
BF16 = jnp.bfloat16


SMEM_IN = pl.BlockSpec(memory_space=pltpu.SMEM)
VMEM_IN = pl.BlockSpec(memory_space=pltpu.VMEM)


HBM_IN = pl.BlockSpec(memory_space=pltpu.HBM)


def in_hbm(array):
    return pltpu.with_memory_space_constraint(array, pltpu.HBM)


def params():
    return pltpu.CompilerParams(vmem_limit_bytes=12 * 1024 * 1024)


def cost(flops, bytes_accessed):
    return pl.CostEstimate(flops=int(flops), bytes_accessed=int(bytes_accessed), transcendentals=0)


def mm(a, b):
    return jnp.dot(a, b, preferred_element_type=F32)


def plan(section, steps, ids_ref, w_ref, sent_ref, k_ref, s_ref, c_ref, m_ref, slots, capacity):
    batches, routes_each, tok = ids_ref.shape
    lanes = k_ref.shape[2]
    picks = routes_each * tok
    sub = lax.broadcasted_iota(jnp.int32, (tok, tok), 0)
    lane = lax.broadcasted_iota(jnp.int32, (tok, tok), 1)
    wide_sub = lax.broadcasted_iota(jnp.int32, (tok, lanes), 0)
    wide_lane = lax.broadcasted_iota(jnp.int32, (tok, lanes), 1)

    def column(values):
        values = jnp.broadcast_to(values, (tok, tok))
        return jnp.sum(jnp.where(sub == lane, values, jnp.zeros_like(values)), axis=1, keepdims=True)

    for step in range(steps):
        m = jnp.clip(step - section, 0, batches - 1)
        ids, weights = ids_ref[m], w_ref[m]
        rows = [ids[k : k + 1] for k in range(routes_each)]
        for k in range(routes_each):
            own = column(rows[k])
            code = own * capacity
            for before in range(k + 1):
                same = own == rows[before]
                if before == k:
                    same &= lane < sub
                code += jnp.sum(jnp.where(same, 1, 0), axis=1, keepdims=True)
            lane_code = jnp.sum(jnp.where(wide_sub == wide_lane % tok, code, 0), axis=0, keepdims=True)
            k_ref[step, k : k + 1, :] = lane_code + wide_lane[:1] // tok * slots
            for b in range(2 * PARTS):
                at = b * picks + k * tok
                hit = code + b * slots == sent_ref[...]
                s_ref[step, at : at + tok, :] = jnp.where(hit, 1.0, 0.0).astype(BF16)
            scale = column(weights[k : k + 1])
            c_ref[step, k * tok : (k + 1) * tok, :] = jnp.broadcast_to(scale, (tok, 128))
        mode = jnp.where(section > step, SENT if step == 1 else TOKENS, COMPUTED)
        mode = jnp.where(section <= step - batches, SENT, mode)
        if step == steps - 1:
            mode = jnp.where(section < SECTIONS - 1, jnp.where(section == 0, TOKENS, SENT), COMPUTED)
        m_ref[step] = jnp.full(m_ref.shape[1:], mode, jnp.int32)


def pack(step, h_ref, g_ref, k_ref, r_ref, o_ref, experts):
    rows = r_ref.shape[0]
    width = o_ref.shape[1]
    piece = rows // experts
    x = h_ref[...].astype(F32)
    scale = lax.rsqrt(jnp.mean(x * x, axis=-1, keepdims=True) + 1e-06)
    normed = (x * scale * g_ref[...]).astype(BF16)
    stack = jnp.concatenate([normed[:, b * width : (b + 1) * width] for b in range(2 * PARTS)], axis=0)
    wanted = k_ref[step]
    hit = r_ref[...] == wanted[:1]
    for k in range(1, wanted.shape[0]):
        hit |= r_ref[...] == wanted[k : k + 1]
    out = mm(jnp.where(hit, 1.0, 0.0).astype(BF16), stack).astype(BF16)
    for e in range(experts):
        for chip in range(2):
            at = (2 * e + chip) * piece
            o_ref[at : at + piece, :] = out[e * piece : (e + 1) * piece]


def begin(place, tokens, gain, row_keys, ids, weights, sent, slots, capacity, experts, steps):
    batches, routes_each, tok = ids.shape
    rows, lanes = row_keys.shape
    picks = routes_each * tok
    full = tokens.shape[1]

    def kernel(place_ref, *refs):
        sources, rest = refs[:6], refs[6:]
        h_ref, g_ref, r_ref, k_ref, s_ref, c_ref, m_ref, o_ref, ids_ref, w_ref, sent_ref, sems = rest
        targets = (h_ref, g_ref, r_ref, ids_ref, w_ref, sent_ref)
        copies = [pltpu.make_async_copy(sources[i], targets[i], sems.at[i]) for i in range(6)]
        for copy in copies:
            copy.start()
        for copy in copies[3:]:
            copy.wait()
        plan(place_ref[0], steps, ids_ref, w_ref, sent_ref, k_ref, s_ref, c_ref, m_ref, slots, capacity)
        for copy in copies[:3]:
            copy.wait()
        pack(0, h_ref, g_ref, k_ref, r_ref, o_ref, experts)

    sources = (tokens, gain, row_keys, ids, weights, sent)
    return pl.pallas_call(
        kernel,
        out_shape=[
            pltpu.VMEM(tokens.shape, BF16),
            pltpu.VMEM(gain.shape, F32),
            pltpu.VMEM(row_keys.shape, jnp.int32),
            pltpu.VMEM((steps, routes_each, lanes), jnp.int32),
            pltpu.VMEM((steps, 2 * PARTS * picks, sent.shape[1]), BF16),
            pltpu.VMEM((steps, picks, 128), F32),
            pltpu.VMEM((steps, 8, 128), jnp.int32),
            jax.ShapeDtypeStruct((2 * rows, full // (2 * PARTS)), BF16),
        ],
        in_specs=[SMEM_IN] + [HBM_IN] * 6,
        out_specs=[VMEM_IN] * 8,
        scratch_shapes=[
            pltpu.VMEM(ids.shape, jnp.int32),
            pltpu.VMEM(weights.shape, F32),
            pltpu.VMEM(sent.shape, jnp.int32),
            pltpu.SemaphoreType.DMA((6,)),
        ],
        compiler_params=params(),
    )(place, *[in_hbm(array) for array in sources])


def front(hidden, gain, keys, row_keys, step, *, width, experts):
    rows, lanes = row_keys.shape

    def kernel(*refs):
        pack(step, *refs, experts)

    return pl.pallas_call(
        kernel,
        out_shape=jax.ShapeDtypeStruct((2 * rows, width), BF16),
        in_specs=[VMEM_IN] * 4,
        out_specs=VMEM_IN,
        compiler_params=params(),
        cost_estimate=cost(2 * rows * lanes * width, 4 * rows * width),
    )(hidden, held(gain), held(keys), held(row_keys))


def held(array):
    return pltpu.with_memory_space_constraint(array, pltpu.VMEM)


def unpack(arrived, perm, part):
    all_rows, width = arrived.shape
    group = perm.shape[0]
    piece = group // PARTS
    some = PARTS // 2

    def kernel(a_ref, p_ref, x_ref):
        chosen = p_ref[part * some * piece : (part + 1) * some * piece, :]
        for g in range(all_rows // group):
            moved = mm(chosen, a_ref[g * group : (g + 1) * group, :]).astype(BF16)
            for b in range(some):
                x_ref[g * piece : (g + 1) * piece, b * width : (b + 1) * width] = moved[b * piece : (b + 1) * piece]

    return pl.pallas_call(
        kernel,
        out_shape=jax.ShapeDtypeStruct((all_rows // PARTS, some * width), BF16),
        in_specs=[VMEM_IN] * 2,
        out_specs=VMEM_IN,
        compiler_params=params(),
        cost_estimate=cost(all_rows * group * width, 3 * all_rows * width),
    )(arrived, perm)


def halves(core, depth):
    own = pl.ds(pl.multiple_of(core * depth, depth), depth)
    other = pl.ds(pl.multiple_of((1 - core) * depth, depth), depth)
    return own, other


def own_half(left, right, gate, up):
    rows, part = left.shape
    units = gate.shape[1]

    def kernel(l_ref, r_ref, g_ref, u_ref, og_ref, ou_ref):
        own_sums(l_ref, r_ref, g_ref, og_ref)
        own_sums(l_ref, r_ref, u_ref, ou_ref)

    return pl.pallas_call(
        kernel,
        out_shape=[jax.ShapeDtypeStruct((rows, units), F32)] * 2,
        in_specs=[VMEM_IN] * 4,
        out_specs=[VMEM_IN] * 2,
        compiler_params=params(),
        cost_estimate=cost(8 * rows * part * units, 8 * part * units),
    )(left, right, held(gate), held(up))


def own_sums(l_ref, r_ref, w_ref, o_ref):
    part = l_ref.shape[1]
    o_ref[...] = mm(l_ref[...], w_ref[:part, :]) + mm(r_ref[...], w_ref[part:, :])


def own_half_staging(place, left, right, gate, up, down, others_down):
    rows, part = left.shape
    depth, units = 2 * part, gate.shape[2]

    def kernel(place_ref, l_ref, r_ref, g_hbm, u_hbm, d_hbm, e_hbm, og_ref, ou_ref, *rest):
        targets, sems = rest[:-1], rest[-1]
        own, other = halves(place_ref[1], depth)
        sources = [hbm.at[0, half, :] for half in (own, other) for hbm in (g_hbm, u_hbm)]
        sources += [hbm.at[0, :, own] for hbm in (d_hbm, e_hbm)]
        copies = [pltpu.make_async_copy(sources[i], targets[i], sems.at[i]) for i in range(6)]
        for copy in copies:
            copy.start()
        copies[0].wait()
        own_sums(l_ref, r_ref, targets[0], og_ref)
        copies[1].wait()
        own_sums(l_ref, r_ref, targets[1], ou_ref)
        for copy in copies[2:]:
            copy.wait()

    return pl.pallas_call(
        kernel,
        out_shape=[jax.ShapeDtypeStruct((rows, units), F32)] * 2
        + [pltpu.VMEM((depth, units), BF16)] * 4
        + [pltpu.VMEM((units, depth), BF16)] * 2,
        in_specs=[SMEM_IN] + [VMEM_IN] * 2 + [HBM_IN] * 4,
        out_specs=[VMEM_IN] * 8,
        scratch_shapes=[pltpu.SemaphoreType.DMA((6,))],
        compiler_params=params(),
        cost_estimate=cost(8 * rows * part * units, 24 * depth * units),
    )(place, left, right, *map(in_hbm, (gate, up, down, others_down)))


def third_quarter(left, gate, up, sum_gate, sum_up):
    rows, part = left.shape
    units = gate.shape[1]

    def kernel(l_ref, g_ref, u_ref, sg_ref, su_ref, og_ref, ou_ref):
        og_ref[...] = sg_ref[...] + mm(l_ref[...], g_ref[:part, :])
        ou_ref[...] = su_ref[...] + mm(l_ref[...], u_ref[:part, :])

    return pl.pallas_call(
        kernel,
        out_shape=[jax.ShapeDtypeStruct((rows, units), F32)] * 2,
        in_specs=[VMEM_IN] * 5,
        out_specs=[VMEM_IN] * 2,
        compiler_params=params(),
        cost_estimate=cost(4 * rows * part * units, 4 * part * units),
    )(left, held(gate), held(up), sum_gate, sum_up)


def last_quarter(right, gate, up, sum_gate, sum_up):
    rows, part = right.shape
    units = gate.shape[1]

    def kernel(r_ref, g_ref, u_ref, sg_ref, su_ref, i_ref):
        pre = sg_ref[...] + mm(r_ref[...], g_ref[part:, :])
        upper = su_ref[...] + mm(r_ref[...], u_ref[part:, :])
        i_ref[...] = (pre * lax.logistic(pre) * upper).astype(BF16)

    return pl.pallas_call(
        kernel,
        out_shape=jax.ShapeDtypeStruct((rows, units), BF16),
        in_specs=[VMEM_IN] * 5,
        out_specs=VMEM_IN,
        compiler_params=params(),
        cost_estimate=cost(4 * rows * part * units, 4 * part * units),
    )(right, held(gate), held(up), sum_gate, sum_up)


def own_units(inner, down):
    rows, units = inner.shape
    depth = down.shape[1]
    piece = depth // PARTS

    def kernel(i_ref, d_ref, o_ref):
        for b in range(PARTS):
            cols = slice(b * piece, (b + 1) * piece)
            o_ref[:, cols] = mm(i_ref[...], d_ref[:, cols])

    return pl.pallas_call(
        kernel,
        out_shape=jax.ShapeDtypeStruct((rows, depth), F32),
        in_specs=[VMEM_IN] * 2,
        out_specs=VMEM_IN,
        compiler_params=params(),
        cost_estimate=cost(2 * rows * units * depth, 2 * units * depth),
    )(inner, held(down))


def other_units(inner, down, total, back, width):
    rows = inner.shape[0]
    group = back.shape[0]
    piece = group // PARTS

    def kernel(i_ref, d_ref, t_ref, q_ref, o_ref, ys):
        for b in range(PARTS):
            cols = slice(b * width, (b + 1) * width)
            ys[b] = (t_ref[:, cols] + mm(i_ref[...], d_ref[:, cols])).astype(BF16)
        for g in range(rows // piece):
            stack = jnp.concatenate([ys[b, g * piece : (g + 1) * piece, :] for b in range(PARTS)], axis=0)
            o_ref[g * group : (g + 1) * group, :] = mm(q_ref[...], stack).astype(BF16)

    return pl.pallas_call(
        kernel,
        out_shape=jax.ShapeDtypeStruct((rows * PARTS, width), BF16),
        in_specs=[VMEM_IN] * 4,
        out_specs=VMEM_IN,
        scratch_shapes=[pltpu.VMEM((PARTS, rows, width), BF16)],
        compiler_params=params(),
        cost_estimate=cost(2 * inner.size * PARTS * width, inner.size),
    )(inner, held(down), total, back)


def combine(returned, spread, scales, modes, hidden, tokens, step):
    rows, width = returned.shape
    tok, full = hidden.shape
    blocks = full // width
    picks = spread.shape[1] // blocks
    routes_each = picks // tok

    def kernel(r_ref, s_ref, w_ref, m_ref, h_ref, t_ref, o_ref):
        got = mm(s_ref[step], r_ref[...])
        scale = w_ref[step][:, :1]
        mode = jnp.broadcast_to(m_ref[step, :1, :1], (tok, 1))
        for b in range(blocks):
            cols = slice(b * width, (b + 1) * width)
            total = h_ref[:, cols].astype(F32)
            for k in range(routes_each):
                at = b * picks + k * tok
                total += scale[k * tok : (k + 1) * tok] * got[at : at + tok]
            for kind, ref in ((TOKENS, t_ref), (SENT, h_ref)):
                total = jnp.where(mode == kind, ref[:, cols].astype(F32), total)
            o_ref[:, cols] = total.astype(BF16)

    return pl.pallas_call(
        kernel,
        out_shape=jax.ShapeDtypeStruct((tok, full), BF16),
        in_specs=[VMEM_IN] * 6,
        out_specs=VMEM_IN,
        compiler_params=params(),
        cost_estimate=cost(2 * spread.shape[1] * rows * width, 2 * rows * width),
    )(returned, held(spread), held(scales), held(modes), hidden, tokens)


def per_device(tokens, norm_gain, gate_weight, up_weight, down_weight, routes, route_weights):
    sections = lax.axis_size("section")
    devices = lax.axis_size("expert")
    experts = devices // SHARDS
    _, batches, tok, routes_each = routes.shape
    full = tokens.shape[2]
    capacity = min(tok, tok * routes_each * 3 // (2 * experts))
    width = full // (2 * PARTS)
    section = lax.axis_index("section")
    core = lax.axis_index("expert") % 2
    place = jnp.stack([section, core]).astype(jnp.int32)

    group = 8 * PARTS * capacity
    at = jnp.arange(group, dtype=jnp.int32)
    wanted = (at % (8 * capacity)) // capacity * (PARTS * capacity) + at // (8 * capacity) * capacity + at % capacity
    perm = (wanted[:, None] == at[None, :]).astype(BF16)
    back = (at[:, None] == wanted[None, :]).astype(BF16)
    place, perm, back = lax.optimization_barrier((place, perm, back))

    slots = experts * capacity
    unit = PARTS * capacity
    row = np.arange(devices * unit // 2)
    row_keys = (row // unit % 2 * PARTS + row % unit // capacity) * slots
    row_keys = row_keys + row // (2 * unit) * capacity + row % capacity
    sent = np.repeat(row_keys.reshape(experts, 1, 2 * unit), 2, axis=1).reshape(1, -1)
    row_keys = np.repeat(row_keys[:, None], 2 * PARTS * tok, axis=1)
    row_keys, sent = jnp.asarray(row_keys, jnp.int32), jnp.asarray(sent, jnp.int32)
    by_route = lambda array: jnp.moveaxis(array[0], 2, 1)
    steps = batches + sections - 1
    own, gain, row_keys, keys, spread, scales, modes, packed = begin(
        place, tokens[0], norm_gain, row_keys, by_route(routes), by_route(route_weights), sent, slots, capacity, experts, steps
    )

    swap = [(i, i ^ 1) for i in range(devices)]
    others_down = lax.ppermute(down_weight, "expert", swap)
    hidden = own
    for step in range(steps):
        if step > 0:
            if step in (1, steps - 1):
                pairs = [(i, i ^ 1) for i in range(sections)]
            else:
                pairs = [(i, (i + 1) % sections) for i in range(sections)]
            hidden = lax.ppermute(current, "section", pairs)
            if step == batches:
                own = hidden
            packed = front(hidden, gain, keys, row_keys, step, width=width, experts=experts)
        arrived = lax.all_to_all(packed, "expert", split_axis=0, concat_axis=0, tiled=True)
        left = unpack(arrived, perm, 0)
        others_left = lax.ppermute(left, "expert", swap)
        right = unpack(arrived, perm, 1)
        others_right = lax.ppermute(right, "expert", swap)
        if step == 0:
            sum_gate, sum_up, gate, up, other_gate, other_up, down, other_down = own_half_staging(
                place, left, right, gate_weight, up_weight, down_weight, others_down
            )
        else:
            sum_gate, sum_up = own_half(left, right, gate, up)
        sum_gate, sum_up = third_quarter(others_left, other_gate, other_up, sum_gate, sum_up)
        inner = last_quarter(others_right, other_gate, other_up, sum_gate, sum_up)
        others_inner = lax.ppermute(inner, "expert", swap)
        total = own_units(inner, down)
        partial_value = other_units(others_inner, other_down, total, back, width)
        returned = lax.all_to_all(partial_value, "expert", split_axis=0, concat_axis=0, tiled=True)
        current = combine(returned, spread, scales, modes, hidden, own, step)
    return current[None]


def solution(mesh):
    return jax.shard_map(
        per_device,
        mesh=mesh,
        in_specs=(
            P("section", "expert", None),
            P("section", None),
            P("section", None, "expert"),
            P("section", None, "expert"),
            P("section", "expert", None),
            P("section", None, "expert", None),
            P("section", None, "expert", None),
        ),
        out_specs=P("section", "expert", None),
        check_vma=False,
    )
```

```python
import jax
import jax.numpy as jnp
import numpy as np
from jax import lax
from jax.experimental import pallas as pl
from jax.experimental.pallas import tpu as pltpu
from jax.sharding import PartitionSpec as P

SHARDS = 4
COMPUTED, TOKENS, SENT = range(3)
SECTIONS = 4
PARTS = 4

F32 = jnp.float32
BF16 = jnp.bfloat16


SMEM_IN = pl.BlockSpec(memory_space=pltpu.SMEM)
VMEM_IN = pl.BlockSpec(memory_space=pltpu.VMEM)


HBM_IN = pl.BlockSpec(memory_space=pltpu.HBM)


def in_hbm(array):
    return pltpu.with_memory_space_constraint(array, pltpu.HBM)


def params():
    return pltpu.CompilerParams(vmem_limit_bytes=12 * 1024 * 1024)


def cost(flops, bytes_accessed):
    return pl.CostEstimate(flops=int(flops), bytes_accessed=int(bytes_accessed), transcendentals=0)


def mm(a, b):
    return jnp.dot(a, b, preferred_element_type=F32)


def slot_codes(section, step, ids_ref, capacity):
    batches, routes_each, tok = ids_ref.shape
    sub = lax.broadcasted_iota(jnp.int32, (tok, tok), 0)
    lane = lax.broadcasted_iota(jnp.int32, (tok, tok), 1)
    ids = ids_ref[jnp.clip(step - section, 0, batches - 1)]
    rows = [ids[k : k + 1] for k in range(routes_each)]
    codes = []
    for k in range(routes_each):
        own = column(rows[k])
        code = own * capacity
        for before in range(k + 1):
            same = own == rows[before]
            if before == k:
                same &= lane < sub
            code += jnp.sum(jnp.where(same, 1, 0), axis=1, keepdims=True)
        codes.append(code)
    return codes


def column(row):
    tok = row.shape[1]
    sub = lax.broadcasted_iota(jnp.int32, (tok, tok), 0)
    lane = lax.broadcasted_iota(jnp.int32, (tok, tok), 1)
    values = jnp.broadcast_to(row, (tok, tok))
    return jnp.sum(jnp.where(sub == lane, values, jnp.zeros_like(values)), axis=1, keepdims=True)


def plan_pack(section, steps, ids_ref, k_ref, slots, capacity):
    tok, lanes = ids_ref.shape[2], k_ref.shape[2]
    sub = lax.broadcasted_iota(jnp.int32, (tok, lanes), 0)
    lane = lax.broadcasted_iota(jnp.int32, (tok, lanes), 1)
    for step in range(steps):
        for k, code in enumerate(slot_codes(section, step, ids_ref, capacity)):
            lane_code = jnp.sum(jnp.where(sub == lane % tok, code, 0), axis=0, keepdims=True)
            k_ref[step, k : k + 1, :] = lane_code + lane[:1] // tok * slots


def plan_combine(section, steps, ids_ref, w_ref, sent_ref, s_ref, c_ref, m_ref, slots, capacity):
    batches, routes_each, tok = ids_ref.shape
    picks = routes_each * tok
    for step in range(steps):
        weights = w_ref[jnp.clip(step - section, 0, batches - 1)]
        for k, code in enumerate(slot_codes(section, step, ids_ref, capacity)):
            for b in range(2 * PARTS):
                at = b * picks + k * tok
                hit = code + b * slots == sent_ref[...]
                s_ref[step, at : at + tok, :] = jnp.where(hit, 1.0, 0.0).astype(BF16)
            scale = column(weights[k : k + 1])
            c_ref[step, k * tok : (k + 1) * tok, :] = jnp.broadcast_to(scale, (tok, 128))
        mode = jnp.where(section > step, SENT if step == 1 else TOKENS, COMPUTED)
        mode = jnp.where(section <= step - batches, SENT, mode)
        if step == steps - 1:
            mode = jnp.where(section < SECTIONS - 1, jnp.where(section == 0, TOKENS, SENT), COMPUTED)
        m_ref[step] = jnp.full(m_ref.shape[1:], mode, jnp.int32)


def pack(step, h_ref, g_ref, k_ref, r_ref, o_ref, experts):
    rows = r_ref.shape[0]
    width = o_ref.shape[1]
    piece = rows // experts
    x = h_ref[...].astype(F32)
    scale = lax.rsqrt(jnp.mean(x * x, axis=-1, keepdims=True) + 1e-06)
    normed = (x * scale * g_ref[...]).astype(BF16)
    stack = jnp.concatenate([normed[:, b * width : (b + 1) * width] for b in range(2 * PARTS)], axis=0)
    wanted = k_ref[step]
    hit = r_ref[...] == wanted[:1]
    for k in range(1, wanted.shape[0]):
        hit |= r_ref[...] == wanted[k : k + 1]
    out = mm(jnp.where(hit, 1.0, 0.0).astype(BF16), stack).astype(BF16)
    for e in range(experts):
        for chip in range(2):
            at = (2 * e + chip) * piece
            o_ref[at : at + piece, :] = out[e * piece : (e + 1) * piece]


def halves(core, depth):
    own = pl.ds(pl.multiple_of(core * depth, depth), depth)
    other = pl.ds(pl.multiple_of((1 - core) * depth, depth), depth)
    return own, other


def begin(place, tokens, gain, row_keys, ids, gate, slots, capacity, experts, steps):
    routes_each = ids.shape[1]
    rows, lanes = row_keys.shape
    full = tokens.shape[1]

    def kernel(place_ref, *refs):
        sources, gate_hbm, rest = refs[:4], refs[4], refs[5:]
        h_ref, g_ref, r_ref, k_ref, o_ref, gate_ref, ids_ref, sems = rest
        own, _ = halves(place_ref[1], full // 2)
        sources += (gate_hbm.at[0, own, :],)
        targets = (h_ref, g_ref, r_ref, ids_ref, gate_ref)
        copies = [pltpu.make_async_copy(sources[i], targets[i], sems.at[i]) for i in range(5)]
        for copy in copies:
            copy.start()
        copies[3].wait()
        plan_pack(place_ref[0], steps, ids_ref, k_ref, slots, capacity)
        for copy in copies[:3]:
            copy.wait()
        pack(0, h_ref, g_ref, k_ref, r_ref, o_ref, experts)
        copies[4].wait()

    sources = (tokens, gain, row_keys, ids, gate)
    return pl.pallas_call(
        kernel,
        out_shape=[
            pltpu.VMEM(tokens.shape, BF16),
            pltpu.VMEM(gain.shape, F32),
            pltpu.VMEM(row_keys.shape, jnp.int32),
            pltpu.VMEM((steps, routes_each, lanes), jnp.int32),
            jax.ShapeDtypeStruct((2 * rows, full // (2 * PARTS)), BF16),
            pltpu.VMEM((full // 2, gate.shape[2]), BF16),
        ],
        in_specs=[SMEM_IN] + [HBM_IN] * 5,
        out_specs=[VMEM_IN] * 6,
        scratch_shapes=[pltpu.VMEM(ids.shape, jnp.int32), pltpu.SemaphoreType.DMA((5,))],
        compiler_params=params(),
    )(place, *[in_hbm(array) for array in sources])


def front(hidden, gain, keys, row_keys, step, *, width, experts):
    rows, lanes = row_keys.shape

    def kernel(*refs):
        pack(step, *refs, experts)

    return pl.pallas_call(
        kernel,
        out_shape=jax.ShapeDtypeStruct((2 * rows, width), BF16),
        in_specs=[VMEM_IN] * 4,
        out_specs=VMEM_IN,
        compiler_params=params(),
        cost_estimate=cost(2 * rows * lanes * width, 4 * rows * width),
    )(hidden, held(gain), held(keys), held(row_keys))


def held(array):
    return pltpu.with_memory_space_constraint(array, pltpu.VMEM)


def unpack(arrived, perm, part):
    all_rows, width = arrived.shape
    group = perm.shape[0]
    piece = group // PARTS
    some = PARTS // 2

    def kernel(a_ref, p_ref, x_ref):
        chosen = p_ref[part * some * piece : (part + 1) * some * piece, :]
        for g in range(all_rows // group):
            moved = mm(chosen, a_ref[g * group : (g + 1) * group, :]).astype(BF16)
            for b in range(some):
                x_ref[g * piece : (g + 1) * piece, b * width : (b + 1) * width] = moved[b * piece : (b + 1) * piece]

    return pl.pallas_call(
        kernel,
        out_shape=jax.ShapeDtypeStruct((all_rows // PARTS, some * width), BF16),
        in_specs=[VMEM_IN] * 2,
        out_specs=VMEM_IN,
        compiler_params=params(),
        cost_estimate=cost(all_rows * group * width, 3 * all_rows * width),
    )(arrived, perm)


def own_half(left, right, gate, up):
    rows, part = left.shape
    units = gate.shape[1]

    def kernel(l_ref, r_ref, g_ref, u_ref, og_ref, ou_ref):
        own_sums(l_ref, r_ref, g_ref, og_ref)
        own_sums(l_ref, r_ref, u_ref, ou_ref)

    return pl.pallas_call(
        kernel,
        out_shape=[jax.ShapeDtypeStruct((rows, units), F32)] * 2,
        in_specs=[VMEM_IN] * 4,
        out_specs=[VMEM_IN] * 2,
        compiler_params=params(),
        cost_estimate=cost(8 * rows * part * units, 8 * part * units),
    )(left, right, held(gate), held(up))


def own_sums(l_ref, r_ref, w_ref, o_ref):
    part = l_ref.shape[1]
    o_ref[...] = mm(l_ref[...], w_ref[:part, :]) + mm(r_ref[...], w_ref[part:, :])


def own_half_staging(place, left, right, own_gate, gate, up, down, others_down, ids, weights, sent, slots, capacity, steps):
    rows, part = left.shape
    depth, units = 2 * part, gate.shape[2]
    picks = ids.shape[1] * ids.shape[2]

    def kernel(place_ref, l_ref, r_ref, own_ref, g_hbm, u_hbm, d_hbm, e_hbm, ids_hbm, w_hbm, sent_hbm, *rest):
        og_ref, ou_ref, *targets, s_ref, c_ref, m_ref, ids_ref, w_ref, sent_ref, sems = rest
        own, other = halves(place_ref[1], depth)
        sources = [ids_hbm, w_hbm, sent_hbm]
        sources += [u_hbm.at[0, own, :], g_hbm.at[0, other, :], u_hbm.at[0, other, :]]
        sources += [hbm.at[0, :, own] for hbm in (d_hbm, e_hbm)]
        targets = [ids_ref, w_ref, sent_ref] + targets
        copies = [pltpu.make_async_copy(sources[i], targets[i], sems.at[i]) for i in range(8)]
        for copy in copies:
            copy.start()
        own_sums(l_ref, r_ref, own_ref, og_ref)
        for copy in copies[:3]:
            copy.wait()
        plan_combine(place_ref[0], steps, ids_ref, w_ref, sent_ref, s_ref, c_ref, m_ref, slots, capacity)
        copies[3].wait()
        own_sums(l_ref, r_ref, targets[3], ou_ref)
        for copy in copies[4:]:
            copy.wait()

    return pl.pallas_call(
        kernel,
        out_shape=[jax.ShapeDtypeStruct((rows, units), F32)] * 2
        + [pltpu.VMEM((depth, units), BF16)] * 3
        + [pltpu.VMEM((units, depth), BF16)] * 2
        + [
            pltpu.VMEM((steps, 2 * PARTS * picks, sent.shape[1]), BF16),
            pltpu.VMEM((steps, picks, 128), F32),
            pltpu.VMEM((steps, 8, 128), jnp.int32),
        ],
        in_specs=[SMEM_IN] + [VMEM_IN] * 3 + [HBM_IN] * 7,
        out_specs=[VMEM_IN] * 10,
        scratch_shapes=[
            pltpu.VMEM(ids.shape, jnp.int32),
            pltpu.VMEM(weights.shape, F32),
            pltpu.VMEM(sent.shape, jnp.int32),
            pltpu.SemaphoreType.DMA((8,)),
        ],
        compiler_params=params(),
        cost_estimate=cost(8 * rows * part * units, 22 * depth * units),
    )(place, left, right, held(own_gate), *map(in_hbm, (gate, up, down, others_down, ids, weights, sent)))


def third_quarter(left, gate, up, sum_gate, sum_up):
    rows, part = left.shape
    units = gate.shape[1]

    def kernel(l_ref, g_ref, u_ref, sg_ref, su_ref, og_ref, ou_ref):
        og_ref[...] = sg_ref[...] + mm(l_ref[...], g_ref[:part, :])
        ou_ref[...] = su_ref[...] + mm(l_ref[...], u_ref[:part, :])

    return pl.pallas_call(
        kernel,
        out_shape=[jax.ShapeDtypeStruct((rows, units), F32)] * 2,
        in_specs=[VMEM_IN] * 5,
        out_specs=[VMEM_IN] * 2,
        compiler_params=params(),
        cost_estimate=cost(4 * rows * part * units, 4 * part * units),
    )(left, held(gate), held(up), sum_gate, sum_up)


def last_quarter(right, gate, up, sum_gate, sum_up):
    rows, part = right.shape
    units = gate.shape[1]

    def kernel(r_ref, g_ref, u_ref, sg_ref, su_ref, i_ref):
        pre = sg_ref[...] + mm(r_ref[...], g_ref[part:, :])
        upper = su_ref[...] + mm(r_ref[...], u_ref[part:, :])
        i_ref[...] = (pre * lax.logistic(pre) * upper).astype(BF16)

    return pl.pallas_call(
        kernel,
        out_shape=jax.ShapeDtypeStruct((rows, units), BF16),
        in_specs=[VMEM_IN] * 5,
        out_specs=VMEM_IN,
        compiler_params=params(),
        cost_estimate=cost(4 * rows * part * units, 4 * part * units),
    )(right, held(gate), held(up), sum_gate, sum_up)


def own_units(inner, down):
    rows, units = inner.shape
    depth = down.shape[1]
    piece = depth // PARTS

    def kernel(i_ref, d_ref, o_ref):
        for b in range(PARTS):
            cols = slice(b * piece, (b + 1) * piece)
            o_ref[:, cols] = mm(i_ref[...], d_ref[:, cols])

    return pl.pallas_call(
        kernel,
        out_shape=jax.ShapeDtypeStruct((rows, depth), F32),
        in_specs=[VMEM_IN] * 2,
        out_specs=VMEM_IN,
        compiler_params=params(),
        cost_estimate=cost(2 * rows * units * depth, 2 * units * depth),
    )(inner, held(down))


def other_units(inner, down, total, back, width):
    rows = inner.shape[0]
    group = back.shape[0]
    piece = group // PARTS

    def kernel(i_ref, d_ref, t_ref, q_ref, o_ref, ys):
        for b in range(PARTS):
            cols = slice(b * width, (b + 1) * width)
            ys[b] = (t_ref[:, cols] + mm(i_ref[...], d_ref[:, cols])).astype(BF16)
        for g in range(rows // piece):
            stack = jnp.concatenate([ys[b, g * piece : (g + 1) * piece, :] for b in range(PARTS)], axis=0)
            o_ref[g * group : (g + 1) * group, :] = mm(q_ref[...], stack).astype(BF16)

    return pl.pallas_call(
        kernel,
        out_shape=jax.ShapeDtypeStruct((rows * PARTS, width), BF16),
        in_specs=[VMEM_IN] * 4,
        out_specs=VMEM_IN,
        scratch_shapes=[pltpu.VMEM((PARTS, rows, width), BF16)],
        compiler_params=params(),
        cost_estimate=cost(2 * inner.size * PARTS * width, inner.size),
    )(inner, held(down), total, back)


def combine(returned, spread, scales, modes, hidden, tokens, step):
    rows, width = returned.shape
    tok, full = hidden.shape
    blocks = full // width
    picks = spread.shape[1] // blocks
    routes_each = picks // tok

    def kernel(r_ref, s_ref, w_ref, m_ref, h_ref, t_ref, o_ref):
        got = mm(s_ref[step], r_ref[...])
        scale = w_ref[step][:, :1]
        mode = jnp.broadcast_to(m_ref[step, :1, :1], (tok, 1))
        for b in range(blocks):
            cols = slice(b * width, (b + 1) * width)
            total = h_ref[:, cols].astype(F32)
            for k in range(routes_each):
                at = b * picks + k * tok
                total += scale[k * tok : (k + 1) * tok] * got[at : at + tok]
            for kind, ref in ((TOKENS, t_ref), (SENT, h_ref)):
                total = jnp.where(mode == kind, ref[:, cols].astype(F32), total)
            o_ref[:, cols] = total.astype(BF16)

    return pl.pallas_call(
        kernel,
        out_shape=jax.ShapeDtypeStruct((tok, full), BF16),
        in_specs=[VMEM_IN] * 6,
        out_specs=VMEM_IN,
        compiler_params=params(),
        cost_estimate=cost(2 * spread.shape[1] * rows * width, 2 * rows * width),
    )(returned, held(spread), held(scales), held(modes), hidden, tokens)


def per_device(tokens, norm_gain, gate_weight, up_weight, down_weight, routes, route_weights):
    sections = lax.axis_size("section")
    devices = lax.axis_size("expert")
    experts = devices // SHARDS
    _, batches, tok, routes_each = routes.shape
    full = tokens.shape[2]
    capacity = min(tok, tok * routes_each * 3 // (2 * experts))
    width = full // (2 * PARTS)
    section = lax.axis_index("section")
    core = lax.axis_index("expert") % 2
    place = jnp.stack([section, core]).astype(jnp.int32)

    group = 8 * PARTS * capacity
    at = jnp.arange(group, dtype=jnp.int32)
    wanted = (at % (8 * capacity)) // capacity * (PARTS * capacity) + at // (8 * capacity) * capacity + at % capacity
    perm = (wanted[:, None] == at[None, :]).astype(BF16)
    back = (at[:, None] == wanted[None, :]).astype(BF16)
    place, perm, back = lax.optimization_barrier((place, perm, back))

    slots = experts * capacity
    unit = PARTS * capacity
    row = np.arange(devices * unit // 2)
    row_keys = (row // unit % 2 * PARTS + row % unit // capacity) * slots
    row_keys = row_keys + row // (2 * unit) * capacity + row % capacity
    sent = np.repeat(row_keys.reshape(experts, 1, 2 * unit), 2, axis=1).reshape(1, -1)
    row_keys = np.repeat(row_keys[:, None], 2 * PARTS * tok, axis=1)
    row_keys, sent = jnp.asarray(row_keys, jnp.int32), jnp.asarray(sent, jnp.int32)
    by_route = lambda array: jnp.moveaxis(array[0], 2, 1)
    steps = batches + sections - 1
    ids, weights = by_route(routes), by_route(route_weights)
    own, gain, row_keys, keys, packed, gate = begin(
        place, tokens[0], norm_gain, row_keys, ids, gate_weight, slots, capacity, experts, steps
    )

    swap = [(i, i ^ 1) for i in range(devices)]
    others_down = lax.ppermute(down_weight, "expert", swap)
    hidden = own
    for step in range(steps):
        if step > 0:
            if step in (1, steps - 1):
                pairs = [(i, i ^ 1) for i in range(sections)]
            else:
                pairs = [(i, (i + 1) % sections) for i in range(sections)]
            hidden = lax.ppermute(current, "section", pairs)
            if step == batches:
                own = hidden
            packed = front(hidden, gain, keys, row_keys, step, width=width, experts=experts)
        arrived = lax.all_to_all(packed, "expert", split_axis=0, concat_axis=0, tiled=True)
        left = unpack(arrived, perm, 0)
        others_left = lax.ppermute(left, "expert", swap)
        right = unpack(arrived, perm, 1)
        others_right = lax.ppermute(right, "expert", swap)
        if step == 0:
            results = own_half_staging(
                place,
                left,
                right,
                gate,
                gate_weight,
                up_weight,
                down_weight,
                others_down,
                ids,
                weights,
                sent,
                slots,
                capacity,
                steps,
            )
            sum_gate, sum_up, up, other_gate, other_up, down, other_down, spread, scales, modes = results
        else:
            sum_gate, sum_up = own_half(left, right, gate, up)
        sum_gate, sum_up = third_quarter(others_left, other_gate, other_up, sum_gate, sum_up)
        inner = last_quarter(others_right, other_gate, other_up, sum_gate, sum_up)
        others_inner = lax.ppermute(inner, "expert", swap)
        total = own_units(inner, down)
        partial_value = other_units(others_inner, other_down, total, back, width)
        returned = lax.all_to_all(partial_value, "expert", split_axis=0, concat_axis=0, tiled=True)
        current = combine(returned, spread, scales, modes, hidden, own, step)
    return current[None]


def solution(mesh):
    return jax.shard_map(
        per_device,
        mesh=mesh,
        in_specs=(
            P("section", "expert", None),
            P("section", None),
            P("section", None, "expert"),
            P("section", None, "expert"),
            P("section", "expert", None),
            P("section", None, "expert", None),
            P("section", None, "expert", None),
        ),
        out_specs=P("section", "expert", None),
        check_vma=False,
    )
```

```python
import jax
import jax.numpy as jnp
import numpy as np
from jax import lax
from jax.experimental import pallas as pl
from jax.experimental.pallas import tpu as pltpu
from jax.sharding import PartitionSpec as P

SHARDS = 4
COMPUTED, TOKENS, SENT = range(3)
SECTIONS = 4
PARTS = 4

F32 = jnp.float32
BF16 = jnp.bfloat16


SMEM_IN = pl.BlockSpec(memory_space=pltpu.SMEM)
VMEM_IN = pl.BlockSpec(memory_space=pltpu.VMEM)


HBM_IN = pl.BlockSpec(memory_space=pltpu.HBM)


def in_hbm(array):
    return pltpu.with_memory_space_constraint(array, pltpu.HBM)


def params():
    return pltpu.CompilerParams(vmem_limit_bytes=12 * 1024 * 1024)


def cost(flops, bytes_accessed):
    return pl.CostEstimate(flops=int(flops), bytes_accessed=int(bytes_accessed), transcendentals=0)


def mm(a, b):
    return jnp.dot(a, b, preferred_element_type=F32)


def slot_codes(section, step, ids_ref, capacity):
    batches, routes_each, tok = ids_ref.shape
    sub = lax.broadcasted_iota(jnp.int32, (tok, tok), 0)
    lane = lax.broadcasted_iota(jnp.int32, (tok, tok), 1)
    ids = ids_ref[jnp.clip(step - section, 0, batches - 1)]
    rows = [ids[k : k + 1] for k in range(routes_each)]
    codes = []
    for k in range(routes_each):
        own = column(rows[k])
        code = own * capacity
        for before in range(k + 1):
            same = own == rows[before]
            if before == k:
                same &= lane < sub
            code += jnp.sum(jnp.where(same, 1, 0), axis=1, keepdims=True)
        codes.append(code)
    return codes


def column(row):
    tok = row.shape[1]
    sub = lax.broadcasted_iota(jnp.int32, (tok, tok), 0)
    lane = lax.broadcasted_iota(jnp.int32, (tok, tok), 1)
    values = jnp.broadcast_to(row, (tok, tok))
    return jnp.sum(jnp.where(sub == lane, values, jnp.zeros_like(values)), axis=1, keepdims=True)


def plan_pack(section, steps, ids_ref, k_ref, slots, capacity):
    tok, lanes = ids_ref.shape[2], k_ref.shape[2]
    sub = lax.broadcasted_iota(jnp.int32, (tok, lanes), 0)
    lane = lax.broadcasted_iota(jnp.int32, (tok, lanes), 1)
    for step in range(steps):
        for k, code in enumerate(slot_codes(section, step, ids_ref, capacity)):
            lane_code = jnp.sum(jnp.where(sub == lane % tok, code, 0), axis=0, keepdims=True)
            k_ref[step, k : k + 1, :] = lane_code + lane[:1] // tok * slots


def plan_combine(section, steps, ids_ref, w_ref, sent_ref, s_ref, c_ref, m_ref, slots, capacity):
    batches, routes_each, tok = ids_ref.shape
    picks = routes_each * tok
    for step in range(steps):
        weights = w_ref[jnp.clip(step - section, 0, batches - 1)]
        for k, code in enumerate(slot_codes(section, step, ids_ref, capacity)):
            for b in range(2 * PARTS):
                at = b * picks + k * tok
                hit = code + b * slots == sent_ref[...]
                s_ref[step, at : at + tok, :] = jnp.where(hit, 1.0, 0.0).astype(BF16)
            scale = column(weights[k : k + 1])
            c_ref[step, k * tok : (k + 1) * tok, :] = jnp.broadcast_to(scale, (tok, 128))
        mode = jnp.where(section > step, SENT if step == 1 else TOKENS, COMPUTED)
        mode = jnp.where(section <= step - batches, SENT, mode)
        if step == steps - 1:
            mode = jnp.where(section < SECTIONS - 1, jnp.where(section == 0, TOKENS, SENT), COMPUTED)
        m_ref[step] = jnp.full(m_ref.shape[1:], mode, jnp.int32)


def pack(step, h_ref, g_ref, k_ref, r_ref, o_ref, experts):
    rows = r_ref.shape[0]
    width = o_ref.shape[1]
    piece = rows // experts
    x = h_ref[...].astype(F32)
    scale = lax.rsqrt(jnp.mean(x * x, axis=-1, keepdims=True) + 1e-06)
    normed = (x * scale * g_ref[...]).astype(BF16)
    stack = jnp.concatenate([normed[:, b * width : (b + 1) * width] for b in range(2 * PARTS)], axis=0)
    wanted = k_ref[step]
    hit = r_ref[...] == wanted[:1]
    for k in range(1, wanted.shape[0]):
        hit |= r_ref[...] == wanted[k : k + 1]
    out = mm(jnp.where(hit, 1.0, 0.0).astype(BF16), stack).astype(BF16)
    for e in range(experts):
        for chip in range(2):
            at = (2 * e + chip) * piece
            o_ref[at : at + piece, :] = out[e * piece : (e + 1) * piece]


def halves(core, depth):
    own = pl.ds(pl.multiple_of(core * depth, depth), depth)
    other = pl.ds(pl.multiple_of((1 - core) * depth, depth), depth)
    return own, other


def begin(place, tokens, gain, row_keys, ids, slots, capacity, experts, steps):
    routes_each = ids.shape[1]
    rows, lanes = row_keys.shape
    full = tokens.shape[1]

    def kernel(place_ref, *refs):
        sources, rest = refs[:4], refs[4:]
        h_ref, g_ref, r_ref, k_ref, o_ref, ids_ref, sems = rest
        targets = (h_ref, g_ref, r_ref, ids_ref)
        copies = [pltpu.make_async_copy(sources[i], targets[i], sems.at[i]) for i in range(4)]
        for copy in copies:
            copy.start()
        copies[3].wait()
        plan_pack(place_ref[0], steps, ids_ref, k_ref, slots, capacity)
        for copy in copies[:3]:
            copy.wait()
        pack(0, h_ref, g_ref, k_ref, r_ref, o_ref, experts)

    sources = (tokens, gain, row_keys, ids)
    return pl.pallas_call(
        kernel,
        out_shape=[
            pltpu.VMEM(tokens.shape, BF16),
            pltpu.VMEM(gain.shape, F32),
            pltpu.VMEM(row_keys.shape, jnp.int32),
            pltpu.VMEM((steps, routes_each, lanes), jnp.int32),
            jax.ShapeDtypeStruct((2 * rows, full // (2 * PARTS)), BF16),
        ],
        in_specs=[SMEM_IN] + [HBM_IN] * 4,
        out_specs=[VMEM_IN] * 5,
        scratch_shapes=[pltpu.VMEM(ids.shape, jnp.int32), pltpu.SemaphoreType.DMA((4,))],
        compiler_params=params(),
    )(place, *[in_hbm(array) for array in sources])


def front(hidden, gain, keys, row_keys, step, *, width, experts):
    rows, lanes = row_keys.shape

    def kernel(*refs):
        pack(step, *refs, experts)

    return pl.pallas_call(
        kernel,
        out_shape=jax.ShapeDtypeStruct((2 * rows, width), BF16),
        in_specs=[VMEM_IN] * 4,
        out_specs=VMEM_IN,
        compiler_params=params(),
        cost_estimate=cost(2 * rows * lanes * width, 4 * rows * width),
    )(hidden, held(gain), held(keys), held(row_keys))


def held(array):
    return pltpu.with_memory_space_constraint(array, pltpu.VMEM)


def unpack(arrived, perm, part):
    all_rows, width = arrived.shape
    group = perm.shape[0]
    piece = group // PARTS
    some = PARTS // 2

    def kernel(a_ref, p_ref, x_ref):
        chosen = p_ref[part * some * piece : (part + 1) * some * piece, :]
        for g in range(all_rows // group):
            moved = mm(chosen, a_ref[g * group : (g + 1) * group, :]).astype(BF16)
            for b in range(some):
                x_ref[g * piece : (g + 1) * piece, b * width : (b + 1) * width] = moved[b * piece : (b + 1) * piece]

    return pl.pallas_call(
        kernel,
        out_shape=jax.ShapeDtypeStruct((all_rows // PARTS, some * width), BF16),
        in_specs=[VMEM_IN] * 2,
        out_specs=VMEM_IN,
        compiler_params=params(),
        cost_estimate=cost(all_rows * group * width, 3 * all_rows * width),
    )(arrived, perm)


def own_half(left, right, gate, up):
    rows, part = left.shape
    units = gate.shape[1]

    def kernel(l_ref, r_ref, g_ref, u_ref, og_ref, ou_ref):
        own_sums(l_ref, r_ref, g_ref, og_ref)
        own_sums(l_ref, r_ref, u_ref, ou_ref)

    return pl.pallas_call(
        kernel,
        out_shape=[jax.ShapeDtypeStruct((rows, units), F32)] * 2,
        in_specs=[VMEM_IN] * 4,
        out_specs=[VMEM_IN] * 2,
        compiler_params=params(),
        cost_estimate=cost(8 * rows * part * units, 8 * part * units),
    )(left, right, held(gate), held(up))


def own_sums(l_ref, r_ref, w_ref, o_ref):
    part = l_ref.shape[1]
    o_ref[...] = mm(l_ref[...], w_ref[:part, :]) + mm(r_ref[...], w_ref[part:, :])


def own_half_staging(place, left, right, gate, up, down, others_down, ids, weights, sent, slots, capacity, steps):
    rows, part = left.shape
    depth, units = 2 * part, gate.shape[2]
    picks = ids.shape[1] * ids.shape[2]

    def kernel(place_ref, l_ref, r_ref, g_hbm, u_hbm, d_hbm, e_hbm, ids_hbm, w_hbm, sent_hbm, *rest):
        og_ref, ou_ref, *targets, s_ref, c_ref, m_ref, ids_ref, w_ref, sent_ref, sems = rest
        own, other = halves(place_ref[1], depth)
        sources = [ids_hbm, w_hbm, sent_hbm]
        sources += [hbm.at[0, half, :] for half in (own, other) for hbm in (g_hbm, u_hbm)]
        sources += [hbm.at[0, :, own] for hbm in (d_hbm, e_hbm)]
        targets = [ids_ref, w_ref, sent_ref] + targets
        copies = [pltpu.make_async_copy(sources[i], targets[i], sems.at[i]) for i in range(9)]
        for copy in copies:
            copy.start()
        for copy in copies[:3]:
            copy.wait()
        plan_combine(place_ref[0], steps, ids_ref, w_ref, sent_ref, s_ref, c_ref, m_ref, slots, capacity)
        for copy, target, sums in zip(copies[3:5], targets[3:5], (og_ref, ou_ref)):
            copy.wait()
            own_sums(l_ref, r_ref, target, sums)
        for copy in copies[5:]:
            copy.wait()

    return pl.pallas_call(
        kernel,
        out_shape=[jax.ShapeDtypeStruct((rows, units), F32)] * 2
        + [pltpu.VMEM((depth, units), BF16)] * 4
        + [pltpu.VMEM((units, depth), BF16)] * 2
        + [
            pltpu.VMEM((steps, 2 * PARTS * picks, sent.shape[1]), BF16),
            pltpu.VMEM((steps, picks, 128), F32),
            pltpu.VMEM((steps, 8, 128), jnp.int32),
        ],
        in_specs=[SMEM_IN] + [VMEM_IN] * 2 + [HBM_IN] * 7,
        out_specs=[VMEM_IN] * 11,
        scratch_shapes=[
            pltpu.VMEM(ids.shape, jnp.int32),
            pltpu.VMEM(weights.shape, F32),
            pltpu.VMEM(sent.shape, jnp.int32),
            pltpu.SemaphoreType.DMA((9,)),
        ],
        compiler_params=params(),
        cost_estimate=cost(8 * rows * part * units, 22 * depth * units),
    )(place, left, right, *map(in_hbm, (gate, up, down, others_down, ids, weights, sent)))


def third_quarter(left, gate, up, sum_gate, sum_up):
    rows, part = left.shape
    units = gate.shape[1]

    def kernel(l_ref, g_ref, u_ref, sg_ref, su_ref, og_ref, ou_ref):
        og_ref[...] = sg_ref[...] + mm(l_ref[...], g_ref[:part, :])
        ou_ref[...] = su_ref[...] + mm(l_ref[...], u_ref[:part, :])

    return pl.pallas_call(
        kernel,
        out_shape=[jax.ShapeDtypeStruct((rows, units), F32)] * 2,
        in_specs=[VMEM_IN] * 5,
        out_specs=[VMEM_IN] * 2,
        compiler_params=params(),
        cost_estimate=cost(4 * rows * part * units, 4 * part * units),
    )(left, held(gate), held(up), sum_gate, sum_up)


def last_quarter(right, gate, up, sum_gate, sum_up):
    rows, part = right.shape
    units = gate.shape[1]

    def kernel(r_ref, g_ref, u_ref, sg_ref, su_ref, i_ref):
        pre = sg_ref[...] + mm(r_ref[...], g_ref[part:, :])
        upper = su_ref[...] + mm(r_ref[...], u_ref[part:, :])
        i_ref[...] = (pre * lax.logistic(pre) * upper).astype(BF16)

    return pl.pallas_call(
        kernel,
        out_shape=jax.ShapeDtypeStruct((rows, units), BF16),
        in_specs=[VMEM_IN] * 5,
        out_specs=VMEM_IN,
        compiler_params=params(),
        cost_estimate=cost(4 * rows * part * units, 4 * part * units),
    )(right, held(gate), held(up), sum_gate, sum_up)


def own_units(inner, down):
    rows, units = inner.shape
    depth = down.shape[1]
    piece = depth // PARTS

    def kernel(i_ref, d_ref, o_ref):
        for b in range(PARTS):
            cols = slice(b * piece, (b + 1) * piece)
            o_ref[:, cols] = mm(i_ref[...], d_ref[:, cols])

    return pl.pallas_call(
        kernel,
        out_shape=jax.ShapeDtypeStruct((rows, depth), F32),
        in_specs=[VMEM_IN] * 2,
        out_specs=VMEM_IN,
        compiler_params=params(),
        cost_estimate=cost(2 * rows * units * depth, 2 * units * depth),
    )(inner, held(down))


def other_units(inner, down, total, back, width):
    rows = inner.shape[0]
    group = back.shape[0]
    piece = group // PARTS

    def kernel(i_ref, d_ref, t_ref, q_ref, o_ref, ys):
        for b in range(PARTS):
            cols = slice(b * width, (b + 1) * width)
            ys[b] = (t_ref[:, cols] + mm(i_ref[...], d_ref[:, cols])).astype(BF16)
        for g in range(rows // piece):
            stack = jnp.concatenate([ys[b, g * piece : (g + 1) * piece, :] for b in range(PARTS)], axis=0)
            o_ref[g * group : (g + 1) * group, :] = mm(q_ref[...], stack).astype(BF16)

    return pl.pallas_call(
        kernel,
        out_shape=jax.ShapeDtypeStruct((rows * PARTS, width), BF16),
        in_specs=[VMEM_IN] * 4,
        out_specs=VMEM_IN,
        scratch_shapes=[pltpu.VMEM((PARTS, rows, width), BF16)],
        compiler_params=params(),
        cost_estimate=cost(2 * inner.size * PARTS * width, inner.size),
    )(inner, held(down), total, back)


def combine(returned, spread, scales, modes, hidden, tokens, step):
    rows, width = returned.shape
    tok, full = hidden.shape
    blocks = full // width
    picks = spread.shape[1] // blocks
    routes_each = picks // tok

    def kernel(r_ref, s_ref, w_ref, m_ref, h_ref, t_ref, o_ref):
        got = mm(s_ref[step], r_ref[...])
        scale = w_ref[step][:, :1]
        mode = jnp.broadcast_to(m_ref[step, :1, :1], (tok, 1))
        for b in range(blocks):
            cols = slice(b * width, (b + 1) * width)
            total = h_ref[:, cols].astype(F32)
            for k in range(routes_each):
                at = b * picks + k * tok
                total += scale[k * tok : (k + 1) * tok] * got[at : at + tok]
            for kind, ref in ((TOKENS, t_ref), (SENT, h_ref)):
                total = jnp.where(mode == kind, ref[:, cols].astype(F32), total)
            o_ref[:, cols] = total.astype(BF16)

    return pl.pallas_call(
        kernel,
        out_shape=jax.ShapeDtypeStruct((tok, full), BF16),
        in_specs=[VMEM_IN] * 6,
        out_specs=VMEM_IN,
        compiler_params=params(),
        cost_estimate=cost(2 * spread.shape[1] * rows * width, 2 * rows * width),
    )(returned, held(spread), held(scales), held(modes), hidden, tokens)


def per_device(tokens, norm_gain, gate_weight, up_weight, down_weight, routes, route_weights):
    sections = lax.axis_size("section")
    devices = lax.axis_size("expert")
    experts = devices // SHARDS
    _, batches, tok, routes_each = routes.shape
    full = tokens.shape[2]
    capacity = min(tok, tok * routes_each * 3 // (2 * experts))
    width = full // (2 * PARTS)
    section = lax.axis_index("section")
    core = lax.axis_index("expert") % 2
    place = jnp.stack([section, core]).astype(jnp.int32)

    group = 8 * PARTS * capacity
    at = jnp.arange(group, dtype=jnp.int32)
    wanted = (at % (8 * capacity)) // capacity * (PARTS * capacity) + at // (8 * capacity) * capacity + at % capacity
    perm = (wanted[:, None] == at[None, :]).astype(BF16)
    back = (at[:, None] == wanted[None, :]).astype(BF16)
    place, perm, back = lax.optimization_barrier((place, perm, back))

    slots = experts * capacity
    unit = PARTS * capacity
    row = np.arange(devices * unit // 2)
    row_keys = (row // unit % 2 * PARTS + row % unit // capacity) * slots
    row_keys = row_keys + row // (2 * unit) * capacity + row % capacity
    sent = np.repeat(row_keys.reshape(experts, 1, 2 * unit), 2, axis=1).reshape(1, -1)
    row_keys = np.repeat(row_keys[:, None], 2 * PARTS * tok, axis=1)
    row_keys, sent = jnp.asarray(row_keys, jnp.int32), jnp.asarray(sent, jnp.int32)
    by_route = lambda array: jnp.moveaxis(array[0], 2, 1)
    steps = batches + sections - 1
    ids, weights = by_route(routes), by_route(route_weights)
    own, gain, row_keys, keys, packed = begin(
        place, tokens[0], norm_gain, row_keys, ids, slots, capacity, experts, steps
    )

    swap = [(i, i ^ 1) for i in range(devices)]
    others_down = lax.ppermute(down_weight, "expert", swap)
    hidden = own
    for step in range(steps):
        if step > 0:
            if step in (1, steps - 1):
                pairs = [(i, i ^ 1) for i in range(sections)]
            else:
                pairs = [(i, (i + 1) % sections) for i in range(sections)]
            hidden = lax.ppermute(current, "section", pairs)
            if step == batches:
                own = hidden
            packed = front(hidden, gain, keys, row_keys, step, width=width, experts=experts)
        arrived = lax.all_to_all(packed, "expert", split_axis=0, concat_axis=0, tiled=True)
        left = unpack(arrived, perm, 0)
        others_left = lax.ppermute(left, "expert", swap)
        right = unpack(arrived, perm, 1)
        others_right = lax.ppermute(right, "expert", swap)
        if step == 0:
            results = own_half_staging(
                place,
                left,
                right,
                gate_weight,
                up_weight,
                down_weight,
                others_down,
                ids,
                weights,
                sent,
                slots,
                capacity,
                steps,
            )
            sum_gate, sum_up, gate, up, other_gate, other_up, down, other_down, spread, scales, modes = results
        else:
            sum_gate, sum_up = own_half(left, right, gate, up)
        sum_gate, sum_up = third_quarter(others_left, other_gate, other_up, sum_gate, sum_up)
        inner = last_quarter(others_right, other_gate, other_up, sum_gate, sum_up)
        others_inner = lax.ppermute(inner, "expert", swap)
        total = own_units(inner, down)
        partial_value = other_units(others_inner, other_down, total, back, width)
        returned = lax.all_to_all(partial_value, "expert", split_axis=0, concat_axis=0, tiled=True)
        current = combine(returned, spread, scales, modes, hidden, own, step)
    return current[None]


def solution(mesh):
    return jax.shard_map(
        per_device,
        mesh=mesh,
        in_specs=(
            P("section", "expert", None),
            P("section", None),
            P("section", None, "expert"),
            P("section", None, "expert"),
            P("section", "expert", None),
            P("section", None, "expert", None),
            P("section", None, "expert", None),
        ),
        out_specs=P("section", "expert", None),
        check_vma=False,
    )
```

```python
import jax
import jax.numpy as jnp
import numpy as np
from jax import lax
from jax.experimental import pallas as pl
from jax.experimental.pallas import tpu as pltpu
from jax.sharding import PartitionSpec as P

SHARDS = 4
COMPUTED, TOKENS, SENT = range(3)
SECTIONS = 4
PARTS = 4

F32 = jnp.float32
BF16 = jnp.bfloat16


SMEM_IN = pl.BlockSpec(memory_space=pltpu.SMEM)
VMEM_IN = pl.BlockSpec(memory_space=pltpu.VMEM)


HBM_IN = pl.BlockSpec(memory_space=pltpu.HBM)


def in_hbm(array):
    return pltpu.with_memory_space_constraint(array, pltpu.HBM)


def params():
    return pltpu.CompilerParams(vmem_limit_bytes=12 * 1024 * 1024)


def cost(flops, bytes_accessed):
    return pl.CostEstimate(flops=int(flops), bytes_accessed=int(bytes_accessed), transcendentals=0)


def mm(a, b):
    return jnp.dot(a, b, preferred_element_type=F32)


def slot_codes(section, step, ids_ref, capacity):
    batches, routes_each, tok = ids_ref.shape
    sub = lax.broadcasted_iota(jnp.int32, (tok, tok), 0)
    lane = lax.broadcasted_iota(jnp.int32, (tok, tok), 1)
    ids = ids_ref[jnp.clip(step - section, 0, batches - 1)]
    rows = [ids[k : k + 1] for k in range(routes_each)]
    codes = []
    for k in range(routes_each):
        own = column(rows[k])
        code = own * capacity
        for before in range(k + 1):
            same = own == rows[before]
            if before == k:
                same &= lane < sub
            code += jnp.sum(jnp.where(same, 1, 0), axis=1, keepdims=True)
        codes.append(code)
    return codes


def column(row):
    tok = row.shape[1]
    sub = lax.broadcasted_iota(jnp.int32, (tok, tok), 0)
    lane = lax.broadcasted_iota(jnp.int32, (tok, tok), 1)
    values = jnp.broadcast_to(row, (tok, tok))
    return jnp.sum(jnp.where(sub == lane, values, jnp.zeros_like(values)), axis=1, keepdims=True)


def plan_pack(section, steps, ids_ref, k_ref, slots, capacity):
    tok, lanes = ids_ref.shape[2], k_ref.shape[2]
    sub = lax.broadcasted_iota(jnp.int32, (tok, lanes), 0)
    lane = lax.broadcasted_iota(jnp.int32, (tok, lanes), 1)
    for step in range(steps):
        for k, code in enumerate(slot_codes(section, step, ids_ref, capacity)):
            lane_code = jnp.sum(jnp.where(sub == lane % tok, code, 0), axis=0, keepdims=True)
            k_ref[step, k : k + 1, :] = lane_code + lane[:1] // tok * slots


def plan_combine(section, steps, ids_ref, w_ref, sent_ref, s_ref, c_ref, m_ref, slots, capacity):
    batches, routes_each, tok = ids_ref.shape
    picks = routes_each * tok
    for step in range(steps):
        weights = w_ref[jnp.clip(step - section, 0, batches - 1)]
        for k, code in enumerate(slot_codes(section, step, ids_ref, capacity)):
            for b in range(2 * PARTS):
                at = b * picks + k * tok
                hit = code + b * slots == sent_ref[...]
                s_ref[step, at : at + tok, :] = jnp.where(hit, 1.0, 0.0).astype(BF16)
            scale = column(weights[k : k + 1])
            c_ref[step, k * tok : (k + 1) * tok, :] = jnp.broadcast_to(scale, (tok, 128))
        mode = jnp.where(section > step, SENT if step == 1 else TOKENS, COMPUTED)
        mode = jnp.where(section <= step - batches, SENT, mode)
        if step == steps - 1:
            mode = jnp.where(section < SECTIONS - 1, jnp.where(section == 0, TOKENS, SENT), COMPUTED)
        m_ref[step] = jnp.full(m_ref.shape[1:], mode, jnp.int32)


def pack(step, h_ref, g_ref, k_ref, r_ref, o_ref, experts):
    rows = r_ref.shape[0]
    width = o_ref.shape[1]
    piece = rows // experts
    x = h_ref[...].astype(F32)
    scale = lax.rsqrt(jnp.mean(x * x, axis=-1, keepdims=True) + 1e-06)
    normed = (x * scale * g_ref[...]).astype(BF16)
    stack = jnp.concatenate([normed[:, b * width : (b + 1) * width] for b in range(2 * PARTS)], axis=0)
    wanted = k_ref[step]
    hit = r_ref[...] == wanted[:1]
    for k in range(1, wanted.shape[0]):
        hit |= r_ref[...] == wanted[k : k + 1]
    out = mm(jnp.where(hit, 1.0, 0.0).astype(BF16), stack).astype(BF16)
    for e in range(experts):
        for chip in range(2):
            at = (2 * e + chip) * piece
            o_ref[at : at + piece, :] = out[e * piece : (e + 1) * piece]


def halves(core, depth):
    own = pl.ds(pl.multiple_of(core * depth, depth), depth)
    other = pl.ds(pl.multiple_of((1 - core) * depth, depth), depth)
    return own, other


def begin(place, tokens, gain, row_keys, ids, slots, capacity, experts, steps):
    routes_each = ids.shape[1]
    rows, lanes = row_keys.shape
    full = tokens.shape[1]

    def kernel(place_ref, *refs):
        sources, rest = refs[:4], refs[4:]
        h_ref, g_ref, r_ref, k_ref, o_ref, ids_ref, sems = rest
        targets = (h_ref, g_ref, r_ref, ids_ref)
        copies = [pltpu.make_async_copy(sources[i], targets[i], sems.at[i]) for i in range(4)]
        for copy in copies:
            copy.start()
        copies[3].wait()
        plan_pack(place_ref[0], steps, ids_ref, k_ref, slots, capacity)
        for copy in copies[:3]:
            copy.wait()
        pack(0, h_ref, g_ref, k_ref, r_ref, o_ref, experts)

    sources = (tokens, gain, row_keys, ids)
    return pl.pallas_call(
        kernel,
        out_shape=[
            pltpu.VMEM(tokens.shape, BF16),
            pltpu.VMEM(gain.shape, F32),
            pltpu.VMEM(row_keys.shape, jnp.int32),
            pltpu.VMEM((steps, routes_each, lanes), jnp.int32),
            jax.ShapeDtypeStruct((2 * rows, full // (2 * PARTS)), BF16),
        ],
        in_specs=[SMEM_IN] + [HBM_IN] * 4,
        out_specs=[VMEM_IN] * 5,
        scratch_shapes=[pltpu.VMEM(ids.shape, jnp.int32), pltpu.SemaphoreType.DMA((4,))],
        compiler_params=params(),
    )(place, *[in_hbm(array) for array in sources])


def front(hidden, gain, keys, row_keys, step, *, width, experts):
    rows, lanes = row_keys.shape

    def kernel(*refs):
        pack(step, *refs, experts)

    return pl.pallas_call(
        kernel,
        out_shape=jax.ShapeDtypeStruct((2 * rows, width), BF16),
        in_specs=[VMEM_IN] * 4,
        out_specs=VMEM_IN,
        compiler_params=params(),
        cost_estimate=cost(2 * rows * lanes * width, 4 * rows * width),
    )(hidden, held(gain), held(keys), held(row_keys))


def held(array):
    return pltpu.with_memory_space_constraint(array, pltpu.VMEM)


def unpack(arrived, perm):
    all_rows, width = arrived.shape
    group = perm.shape[0]
    piece = group // PARTS
    some = PARTS // 2

    def kernel(a_ref, p_ref, *halved):
        for g in range(all_rows // group):
            moved = mm(p_ref[...], a_ref[g * group : (g + 1) * group, :]).astype(BF16)
            for b in range(PARTS):
                x_ref, at = halved[b // some], b % some * width
                x_ref[g * piece : (g + 1) * piece, at : at + width] = moved[b * piece : (b + 1) * piece]

    return pl.pallas_call(
        kernel,
        out_shape=[jax.ShapeDtypeStruct((all_rows // PARTS, some * width), BF16)] * 2,
        in_specs=[VMEM_IN] * 2,
        out_specs=[VMEM_IN] * 2,
        compiler_params=params(),
        cost_estimate=cost(all_rows * group * width, 3 * all_rows * width),
    )(arrived, perm)


def own_half(left, right, gate, up):
    rows, part = left.shape
    units = gate.shape[1]

    def kernel(l_ref, r_ref, g_ref, u_ref, og_ref, ou_ref):
        own_sums(l_ref, r_ref, g_ref, og_ref)
        own_sums(l_ref, r_ref, u_ref, ou_ref)

    return pl.pallas_call(
        kernel,
        out_shape=[jax.ShapeDtypeStruct((rows, units), F32)] * 2,
        in_specs=[VMEM_IN] * 4,
        out_specs=[VMEM_IN] * 2,
        compiler_params=params(),
        cost_estimate=cost(8 * rows * part * units, 8 * part * units),
    )(left, right, held(gate), held(up))


def own_sums(l_ref, r_ref, w_ref, o_ref):
    part = l_ref.shape[1]
    o_ref[...] = mm(l_ref[...], w_ref[:part, :]) + mm(r_ref[...], w_ref[part:, :])


def own_half_staging(place, left, right, gate, up, down, others_down, ids, weights, sent, slots, capacity, steps):
    rows, part = left.shape
    depth, units = 2 * part, gate.shape[2]
    picks = ids.shape[1] * ids.shape[2]

    def kernel(place_ref, l_ref, r_ref, g_hbm, u_hbm, d_hbm, e_hbm, ids_hbm, w_hbm, sent_hbm, *rest):
        og_ref, ou_ref, *targets, s_ref, c_ref, m_ref, ids_ref, w_ref, sent_ref, sems = rest
        own, other = halves(place_ref[1], depth)
        sources = [ids_hbm, w_hbm, sent_hbm]
        sources += [hbm.at[0, half, :] for half in (own, other) for hbm in (g_hbm, u_hbm)]
        sources += [hbm.at[0, :, own] for hbm in (d_hbm, e_hbm)]
        targets = [ids_ref, w_ref, sent_ref] + targets
        copies = [pltpu.make_async_copy(sources[i], targets[i], sems.at[i]) for i in range(9)]
        for copy in copies:
            copy.start()
        for copy in copies[:3]:
            copy.wait()
        plan_combine(place_ref[0], steps, ids_ref, w_ref, sent_ref, s_ref, c_ref, m_ref, slots, capacity)
        for copy, target, sums in zip(copies[3:5], targets[3:5], (og_ref, ou_ref)):
            copy.wait()
            own_sums(l_ref, r_ref, target, sums)
        for copy in copies[5:]:
            copy.wait()

    return pl.pallas_call(
        kernel,
        out_shape=[jax.ShapeDtypeStruct((rows, units), F32)] * 2
        + [pltpu.VMEM((depth, units), BF16)] * 4
        + [pltpu.VMEM((units, depth), BF16)] * 2
        + [
            pltpu.VMEM((steps, 2 * PARTS * picks, sent.shape[1]), BF16),
            pltpu.VMEM((steps, picks, 128), F32),
            pltpu.VMEM((steps, 8, 128), jnp.int32),
        ],
        in_specs=[SMEM_IN] + [VMEM_IN] * 2 + [HBM_IN] * 7,
        out_specs=[VMEM_IN] * 11,
        scratch_shapes=[
            pltpu.VMEM(ids.shape, jnp.int32),
            pltpu.VMEM(weights.shape, F32),
            pltpu.VMEM(sent.shape, jnp.int32),
            pltpu.SemaphoreType.DMA((9,)),
        ],
        compiler_params=params(),
        cost_estimate=cost(8 * rows * part * units, 22 * depth * units),
    )(place, left, right, *map(in_hbm, (gate, up, down, others_down, ids, weights, sent)))


def third_quarter(left, gate, up, sum_gate, sum_up):
    rows, part = left.shape
    units = gate.shape[1]

    def kernel(l_ref, g_ref, u_ref, sg_ref, su_ref, og_ref, ou_ref):
        og_ref[...] = sg_ref[...] + mm(l_ref[...], g_ref[:part, :])
        ou_ref[...] = su_ref[...] + mm(l_ref[...], u_ref[:part, :])

    return pl.pallas_call(
        kernel,
        out_shape=[jax.ShapeDtypeStruct((rows, units), F32)] * 2,
        in_specs=[VMEM_IN] * 5,
        out_specs=[VMEM_IN] * 2,
        compiler_params=params(),
        cost_estimate=cost(4 * rows * part * units, 4 * part * units),
    )(left, held(gate), held(up), sum_gate, sum_up)


def last_quarter(right, gate, up, sum_gate, sum_up):
    rows, part = right.shape
    units = gate.shape[1]

    def kernel(r_ref, g_ref, u_ref, sg_ref, su_ref, i_ref):
        pre = sg_ref[...] + mm(r_ref[...], g_ref[part:, :])
        upper = su_ref[...] + mm(r_ref[...], u_ref[part:, :])
        i_ref[...] = (pre * lax.logistic(pre) * upper).astype(BF16)

    return pl.pallas_call(
        kernel,
        out_shape=jax.ShapeDtypeStruct((rows, units), BF16),
        in_specs=[VMEM_IN] * 5,
        out_specs=VMEM_IN,
        compiler_params=params(),
        cost_estimate=cost(4 * rows * part * units, 4 * part * units),
    )(right, held(gate), held(up), sum_gate, sum_up)


def own_units(inner, down):
    rows, units = inner.shape
    depth = down.shape[1]
    piece = depth // PARTS

    def kernel(i_ref, d_ref, o_ref):
        for b in range(PARTS):
            cols = slice(b * piece, (b + 1) * piece)
            o_ref[:, cols] = mm(i_ref[...], d_ref[:, cols])

    return pl.pallas_call(
        kernel,
        out_shape=jax.ShapeDtypeStruct((rows, depth), F32),
        in_specs=[VMEM_IN] * 2,
        out_specs=VMEM_IN,
        compiler_params=params(),
        cost_estimate=cost(2 * rows * units * depth, 2 * units * depth),
    )(inner, held(down))


def other_units(inner, down, total, back, width):
    rows = inner.shape[0]
    group = back.shape[0]
    piece = group // PARTS

    def kernel(i_ref, d_ref, t_ref, q_ref, o_ref, ys):
        for b in range(PARTS):
            cols = slice(b * width, (b + 1) * width)
            ys[b] = (t_ref[:, cols] + mm(i_ref[...], d_ref[:, cols])).astype(BF16)
        for g in range(rows // piece):
            stack = jnp.concatenate([ys[b, g * piece : (g + 1) * piece, :] for b in range(PARTS)], axis=0)
            o_ref[g * group : (g + 1) * group, :] = mm(q_ref[...], stack).astype(BF16)

    return pl.pallas_call(
        kernel,
        out_shape=jax.ShapeDtypeStruct((rows * PARTS, width), BF16),
        in_specs=[VMEM_IN] * 4,
        out_specs=VMEM_IN,
        scratch_shapes=[pltpu.VMEM((PARTS, rows, width), BF16)],
        compiler_params=params(),
        cost_estimate=cost(2 * inner.size * PARTS * width, inner.size),
    )(inner, held(down), total, back)


def combine(returned, spread, scales, modes, hidden, tokens, step):
    rows, width = returned.shape
    tok, full = hidden.shape
    blocks = full // width
    picks = spread.shape[1] // blocks
    routes_each = picks // tok

    def kernel(r_ref, s_ref, w_ref, m_ref, h_ref, t_ref, o_ref):
        got = mm(s_ref[step], r_ref[...])
        scale = w_ref[step][:, :1]
        mode = jnp.broadcast_to(m_ref[step, :1, :1], (tok, 1))
        for b in range(blocks):
            cols = slice(b * width, (b + 1) * width)
            total = h_ref[:, cols].astype(F32)
            for k in range(routes_each):
                at = b * picks + k * tok
                total += scale[k * tok : (k + 1) * tok] * got[at : at + tok]
            for kind, ref in ((TOKENS, t_ref), (SENT, h_ref)):
                total = jnp.where(mode == kind, ref[:, cols].astype(F32), total)
            o_ref[:, cols] = total.astype(BF16)

    return pl.pallas_call(
        kernel,
        out_shape=jax.ShapeDtypeStruct((tok, full), BF16),
        in_specs=[VMEM_IN] * 6,
        out_specs=VMEM_IN,
        compiler_params=params(),
        cost_estimate=cost(2 * spread.shape[1] * rows * width, 2 * rows * width),
    )(returned, held(spread), held(scales), held(modes), hidden, tokens)


def per_device(tokens, norm_gain, gate_weight, up_weight, down_weight, routes, route_weights):
    sections = lax.axis_size("section")
    devices = lax.axis_size("expert")
    experts = devices // SHARDS
    _, batches, tok, routes_each = routes.shape
    full = tokens.shape[2]
    capacity = min(tok, tok * routes_each * 3 // (2 * experts))
    width = full // (2 * PARTS)
    section = lax.axis_index("section")
    core = lax.axis_index("expert") % 2
    place = jnp.stack([section, core]).astype(jnp.int32)

    group = 8 * PARTS * capacity
    at = jnp.arange(group, dtype=jnp.int32)
    wanted = (at % (8 * capacity)) // capacity * (PARTS * capacity) + at // (8 * capacity) * capacity + at % capacity
    perm = (wanted[:, None] == at[None, :]).astype(BF16)
    back = (at[:, None] == wanted[None, :]).astype(BF16)
    place, perm, back = lax.optimization_barrier((place, perm, back))

    slots = experts * capacity
    unit = PARTS * capacity
    row = np.arange(devices * unit // 2)
    row_keys = (row // unit % 2 * PARTS + row % unit // capacity) * slots
    row_keys = row_keys + row // (2 * unit) * capacity + row % capacity
    sent = np.repeat(row_keys.reshape(experts, 1, 2 * unit), 2, axis=1).reshape(1, -1)
    row_keys = np.repeat(row_keys[:, None], 2 * PARTS * tok, axis=1)
    row_keys, sent = jnp.asarray(row_keys, jnp.int32), jnp.asarray(sent, jnp.int32)
    by_route = lambda array: jnp.moveaxis(array[0], 2, 1)
    steps = batches + sections - 1
    ids, weights = by_route(routes), by_route(route_weights)
    own, gain, row_keys, keys, packed = begin(
        place, tokens[0], norm_gain, row_keys, ids, slots, capacity, experts, steps
    )

    swap = [(i, i ^ 1) for i in range(devices)]
    others_down = lax.ppermute(down_weight, "expert", swap)
    hidden = own
    for step in range(steps):
        if step > 0:
            if step in (1, steps - 1):
                pairs = [(i, i ^ 1) for i in range(sections)]
            else:
                pairs = [(i, (i + 1) % sections) for i in range(sections)]
            hidden = lax.ppermute(current, "section", pairs)
            if step == batches:
                own = hidden
            packed = front(hidden, gain, keys, row_keys, step, width=width, experts=experts)
        arrived = lax.all_to_all(packed, "expert", split_axis=0, concat_axis=0, tiled=True)
        left, right = unpack(arrived, perm)
        others_left = lax.ppermute(left, "expert", swap)
        others_right = lax.ppermute(right, "expert", swap)
        if step == 0:
            results = own_half_staging(
                place,
                left,
                right,
                gate_weight,
                up_weight,
                down_weight,
                others_down,
                ids,
                weights,
                sent,
                slots,
                capacity,
                steps,
            )
            sum_gate, sum_up, gate, up, other_gate, other_up, down, other_down, spread, scales, modes = results
        else:
            sum_gate, sum_up = own_half(left, right, gate, up)
        sum_gate, sum_up = third_quarter(others_left, other_gate, other_up, sum_gate, sum_up)
        inner = last_quarter(others_right, other_gate, other_up, sum_gate, sum_up)
        others_inner = lax.ppermute(inner, "expert", swap)
        total = own_units(inner, down)
        partial_value = other_units(others_inner, other_down, total, back, width)
        returned = lax.all_to_all(partial_value, "expert", split_axis=0, concat_axis=0, tiled=True)
        current = combine(returned, spread, scales, modes, hidden, own, step)
    return current[None]


def solution(mesh):
    return jax.shard_map(
        per_device,
        mesh=mesh,
        in_specs=(
            P("section", "expert", None),
            P("section", None),
            P("section", None, "expert"),
            P("section", None, "expert"),
            P("section", "expert", None),
            P("section", None, "expert", None),
            P("section", None, "expert", None),
        ),
        out_specs=P("section", "expert", None),
        check_vma=False,
    )
```
